256 devices in a mesh: ctx: 64 (over z, y, x_lo), head: 4 (over x_hi, core).
Axes of the slice: x: 4 (x_hi: 2, x_lo: 2; x = x_hi * 2 + x_lo), y: 4, z: 8, core: 2. Of those that a mesh axis runs over, the one named last changes fastest.
Arguments:
- queries: bfloat16 [32768, 4096], P(('ctx', 'head')), may hold values from -6 to 6
- keys: bfloat16 [32768, 1024], P(('ctx', 'head')), may hold values from -6 to 6
- values: bfloat16 [32768, 1024], P(('ctx', 'head')), may hold values from -6 to 6
- cotangent: bfloat16 [32768, 4096], P(('ctx', 'head')), may hold values from -6 to 6
Outputs:
- out: bfloat16 [32768, 4096], P(('ctx', 'head'))
- grad_queries: bfloat16 [32768, 4096], P(('ctx', 'head'))
- grad_keys: bfloat16 [32768, 1024], P(('ctx', 'head'))
- grad_values: bfloat16 [32768, 1024], P(('ctx', 'head'))
The draws below stay inside these ranges and needn't reach their ends.
All inputs are finite; a program needn't handle non-finite values.
Results may differ from the reference program's by a relative error of at most 0.008.
Values may be sent and summed in bfloat16 or wider, within the bound.
A program may use at most 64 MiB of HBM per device.

```python
from functools import partial
import jax
import jax.numpy as jnp
from jax import lax

QUERY_HEADS = 32
KEY_VALUE_HEADS = 8
HEAD_FEATURES = 128
BLOCK_POSITIONS = 512
BLOCK_COUNT = 64
SEQUENCE_LENGTH = 32768


def draw_queries(key, part):
    layer_output = jax.random.normal(jax.random.fold_in(key, 3), (SEQUENCE_LENGTH, QUERY_HEADS, HEAD_FEATURES), jnp.float32)
    return jnp.clip(layer_output, -6.0, 6.0).reshape(SEQUENCE_LENGTH, QUERY_HEADS * HEAD_FEATURES).astype(jnp.bfloat16)


def draw_keys(key, part):
    random_noise = jax.random.normal(jax.random.fold_in(key, 1), (BLOCK_COUNT, BLOCK_POSITIONS, KEY_VALUE_HEADS, HEAD_FEATURES), jnp.float32)
    start_offset = 2.0 * jax.random.normal(jax.random.fold_in(key, 2), (BLOCK_COUNT, 1, KEY_VALUE_HEADS, HEAD_FEATURES), jnp.float32)
    layer_output = (random_noise + start_offset).reshape(SEQUENCE_LENGTH, KEY_VALUE_HEADS, HEAD_FEATURES)
    return jnp.clip(layer_output, -6.0, 6.0).reshape(SEQUENCE_LENGTH, KEY_VALUE_HEADS * HEAD_FEATURES).astype(jnp.bfloat16)


def draw_values(key, part):
    random_noise = jax.random.normal(jax.random.fold_in(key, 6), (BLOCK_COUNT, BLOCK_POSITIONS, KEY_VALUE_HEADS, HEAD_FEATURES), jnp.float32)
    start_offset = jax.random.normal(jax.random.fold_in(key, 7), (BLOCK_COUNT, 1, KEY_VALUE_HEADS, HEAD_FEATURES), jnp.float32)
    layer_output = random_noise + start_offset
    return jnp.clip(layer_output, -6.0, 6.0).reshape(SEQUENCE_LENGTH, KEY_VALUE_HEADS * HEAD_FEATURES).astype(jnp.bfloat16)


def levels(rng, extent, cuts, least, high):
    def one(dim, shards_of):
        steps = jax.random.uniform(jax.random.fold_in(jax.random.fold_in(rng, 6), dim), (shards_of,), jnp.float32, least / len(cuts), high / len(cuts))
        return jnp.repeat(jnp.exp(steps), extent[dim] // shards_of).reshape((-1,) + (1,) * (len(extent) - dim - 1))

    gain = one(*cuts[0])
    for cut in cuts[1:]:
        gain = gain * one(*cut)
    return gain


def centred(own_key, shape, scale, most, cuts=(), held_as=jnp.bfloat16):
    entries = jax.random.normal(own_key, shape, jnp.float32) * scale
    if len(cuts) > 0:
        entries = levels(own_key, shape, cuts, -0.22, 0.18) * entries
    return jnp.clip(entries, min=-most, max=most).astype(held_as)


def setup_inputs(seed: int = 0) -> dict:
    key_list = jax.random.split(jax.random.key(seed), 5)
    queries = draw_queries(jax.random.fold_in(key_list[4], 71), 0)
    keys = draw_keys(jax.random.fold_in(key_list[4], 71), 0)
    values = draw_values(jax.random.fold_in(key_list[4], 71), 0)
    cotangent = centred(key_list[3], (SEQUENCE_LENGTH, QUERY_HEADS * HEAD_FEATURES), 1.0, 6.0, ((0, 256),))
    return dict(queries=queries, keys=keys, values=values, cotangent=cotangent)


LOWEST = -1e30


def head_terms(query, grad_out, band_keys, band_values, block_summary_keys, block_summary_values, first, keep):
    row_count = query.shape[0]
    width = band_keys.shape[0]
    scale = query.shape[1] ** -0.5
    query_pos = first + jnp.arange(row_count, dtype=jnp.int32)
    key_pos = first - (width - row_count) + jnp.arange(width, dtype=jnp.int32)
    band_mask = (key_pos[None, :] >= 0) & (key_pos[None, :] <= query_pos[:, None])
    summary_mask = jnp.arange(block_summary_keys.shape[0], dtype=jnp.int32)[None, :] < (first // BLOCK_POSITIONS)
    band_score = jnp.dot(query, band_keys.T, preferred_element_type=jnp.float32) * scale
    summary_score = jnp.dot(query, block_summary_keys.T, preferred_element_type=jnp.float32) * scale
    row_top = jnp.maximum(jnp.max(jnp.where(band_mask, band_score, LOWEST), axis=1),
                          jnp.max(jnp.where(summary_mask, summary_score, LOWEST), axis=1))
    band_weight = jnp.where(band_mask, jnp.exp(band_score - row_top[:, None]), 0.0)
    summary_weight = jnp.where(summary_mask, jnp.exp(summary_score - row_top[:, None]), 0.0)
    row_total = jnp.sum(band_weight, axis=1) + jnp.sum(summary_weight, axis=1)
    band_prob = band_weight / row_total[:, None]
    summary_prob = summary_weight / row_total[:, None]
    band_low = band_prob.astype(jnp.bfloat16)
    summary_low = summary_prob.astype(jnp.bfloat16)
    attended = jnp.dot(band_low, band_values, preferred_element_type=jnp.float32) + jnp.dot(summary_low, block_summary_values, preferred_element_type=jnp.float32)
    row_dot = jnp.sum(grad_out.astype(jnp.float32) * attended, axis=1)
    band_back = jnp.dot(grad_out, band_values.T, preferred_element_type=jnp.float32)
    summary_back = jnp.dot(grad_out, block_summary_values.T, preferred_element_type=jnp.float32)
    band_slope = (band_prob * (band_back - row_dot[:, None])).astype(jnp.bfloat16)
    summary_slope = (summary_prob * (summary_back - row_dot[:, None])).astype(jnp.bfloat16)
    grad_query = (jnp.dot(band_slope, band_keys, preferred_element_type=jnp.float32) + jnp.dot(summary_slope, block_summary_keys, preferred_element_type=jnp.float32)) * scale
    grad_key = jnp.dot(band_slope[:, width - keep:].T, query, preferred_element_type=jnp.float32) * scale
    grad_value = jnp.dot(band_low[:, width - keep:].T, grad_out, preferred_element_type=jnp.float32)
    grad_sum_key = jnp.dot(summary_slope.T, query, preferred_element_type=jnp.float32) * scale
    grad_sum_value = jnp.dot(summary_low.T, grad_out, preferred_element_type=jnp.float32)
    return attended, grad_query, grad_key, grad_value, grad_sum_key, grad_sum_value, row_top, row_total, row_dot


def combine_blocks(band_all, summary_total):
    own = band_all[:, :, BLOCK_POSITIONS:]
    later = jnp.concatenate([band_all[1:, :, :BLOCK_POSITIONS], jnp.zeros_like(band_all[:1, :, :BLOCK_POSITIONS])], axis=0)
    spread = summary_total.transpose(1, 0, 2)[:, :, None, :] / BLOCK_POSITIONS
    grand_total = own + later + spread
    return grand_total.transpose(0, 2, 1, 3).reshape(SEQUENCE_LENGTH, KEY_VALUE_HEADS * HEAD_FEATURES).astype(jnp.bfloat16)


def reference(queries, keys, values, cotangent):
    head_count = QUERY_HEADS // KEY_VALUE_HEADS
    query_blocks = queries.reshape(BLOCK_COUNT, BLOCK_POSITIONS, QUERY_HEADS, HEAD_FEATURES)
    scaled_blocks = (cotangent * 16).astype(jnp.bfloat16).reshape(BLOCK_COUNT, BLOCK_POSITIONS, QUERY_HEADS, HEAD_FEATURES)
    token_keys = keys.reshape(SEQUENCE_LENGTH, KEY_VALUE_HEADS, HEAD_FEATURES)
    token_values = values.reshape(SEQUENCE_LENGTH, KEY_VALUE_HEADS, HEAD_FEATURES)
    block_summary_keys = (jnp.sum(token_keys.reshape(BLOCK_COUNT, BLOCK_POSITIONS, KEY_VALUE_HEADS, HEAD_FEATURES), axis=1, dtype=jnp.float32) / BLOCK_POSITIONS).astype(jnp.bfloat16)
    block_summary_values = (jnp.sum(token_values.reshape(BLOCK_COUNT, BLOCK_POSITIONS, KEY_VALUE_HEADS, HEAD_FEATURES), axis=1, dtype=jnp.float32) / BLOCK_POSITIONS).astype(jnp.bfloat16)
    summary_key_heads = jnp.repeat(block_summary_keys.transpose(1, 0, 2), head_count, axis=0)
    summary_value_heads = jnp.repeat(block_summary_values.transpose(1, 0, 2), head_count, axis=0)
    pad_amount = jnp.zeros((BLOCK_POSITIONS, KEY_VALUE_HEADS, HEAD_FEATURES), jnp.bfloat16)
    padded_keys = jnp.concatenate([pad_amount, token_keys], axis=0)
    padded_values = jnp.concatenate([pad_amount, token_values], axis=0)

    def step_block(carry, block):
        key_running_sum, value_running_sum = carry
        first = block * BLOCK_POSITIONS
        band_keys = lax.dynamic_slice_in_dim(padded_keys, first, 2 * BLOCK_POSITIONS, 0)
        band_values = lax.dynamic_slice_in_dim(padded_values, first, 2 * BLOCK_POSITIONS, 0)
        band_key_heads = jnp.repeat(band_keys.transpose(1, 0, 2), head_count, axis=0)
        band_value_heads = jnp.repeat(band_values.transpose(1, 0, 2), head_count, axis=0)
        query_heads = lax.dynamic_index_in_dim(query_blocks, block, 0, keepdims=False).transpose(1, 0, 2)
        grad_heads = lax.dynamic_index_in_dim(scaled_blocks, block, 0, keepdims=False).transpose(1, 0, 2)
        term_list = jax.vmap(partial(head_terms, first=first, keep=2 * BLOCK_POSITIONS))(
            query_heads, grad_heads, band_key_heads, band_value_heads, summary_key_heads, summary_value_heads)
        key_running_sum = key_running_sum + term_list[4].reshape(KEY_VALUE_HEADS, head_count, BLOCK_COUNT, HEAD_FEATURES).sum(axis=1)
        value_running_sum = value_running_sum + term_list[5].reshape(KEY_VALUE_HEADS, head_count, BLOCK_COUNT, HEAD_FEATURES).sum(axis=1)
        local_key_gradient = term_list[2].reshape(KEY_VALUE_HEADS, head_count, 2 * BLOCK_POSITIONS, HEAD_FEATURES).sum(axis=1)
        local_value_gradient = term_list[3].reshape(KEY_VALUE_HEADS, head_count, 2 * BLOCK_POSITIONS, HEAD_FEATURES).sum(axis=1)
        return (key_running_sum, value_running_sum), (term_list[0].astype(jnp.bfloat16), term_list[1].astype(jnp.bfloat16), local_key_gradient, local_value_gradient)

    initial_state = (jnp.zeros((KEY_VALUE_HEADS, BLOCK_COUNT, HEAD_FEATURES), jnp.float32), jnp.zeros((KEY_VALUE_HEADS, BLOCK_COUNT, HEAD_FEATURES), jnp.float32))
    (key_running_sum, value_running_sum), (out_all, grad_query_all, band_key_all, band_value_all) = lax.scan(
        step_block, initial_state, jnp.arange(BLOCK_COUNT, dtype=jnp.int32))
    out = out_all.transpose(0, 2, 1, 3).reshape(SEQUENCE_LENGTH, QUERY_HEADS * HEAD_FEATURES)
    grad_queries = grad_query_all.transpose(0, 2, 1, 3).reshape(SEQUENCE_LENGTH, QUERY_HEADS * HEAD_FEATURES)
    grad_keys = combine_blocks(band_key_all, key_running_sum)
    grad_values = combine_blocks(band_value_all, value_running_sum)
    return (out, grad_queries, grad_keys, grad_values)
```

```python
import math

import jax
import jax.numpy as jnp
from jax import lax
from jax.experimental import pallas as pl
from jax.experimental.pallas import tpu as pltpu
from jax.sharding import PartitionSpec as P

MESH = pl.DeviceIdType.MESH
F32 = jnp.float32
BF16 = jnp.bfloat16

D = 128
BLOCK = 512
ROWS = 128
CHIP = 256
GROUPS = 4
REPEAT = 4
KCOLS = GROUPS * D
QCOLS = GROUPS * REPEAT * D
BAND = 4 * CHIP
NX, NY, NZ = 4, 4, 8
NCTX = 64
LOWEST = -1e30
SCALE = 1.0 / math.sqrt(D)
LOG2 = SCALE / math.log(2.0)


def dot(a, b):
    return jnp.dot(a, b, preferred_element_type=F32)


def dot_t(a, b):
    return lax.dot_general(a, b, (((1,), (1,)), ((), ())), preferred_element_type=F32)


def al(index, size):
    return pl.multiple_of(index * size, size)


def kernel(
    q_in, k_in, v_in, do_in, out_ref, gq_ref, gk_ref, gv_ref,
    qb, dob, kv, kvt, probs, ob, gqb, db, stats, outb, gqout,
    xs, sumb, sg, rsz, rsy, rsx, acc1, acc2, acc3,
    dkv, own, gsend, grecv, fin,
    kv_send, kv_recv, q_send, do_send, q_recv, do_recv,
    xs_send, xs_recv, ys_send, ys_recv, zs_send, zs_recv,
    rz_send, rz_recv, ry_send, ry_recv, rx_send, rx_recv,
    g_send, g_recv, o_send, o_recv, o_local, f_send, f_recv, f_local,
):
    ctx = lax.axis_index("ctx")
    head = lax.axis_index("head")
    core = lax.rem(head, 2)
    xh = lax.div(head, 2)
    xl = lax.rem(ctx, 2)
    y = lax.rem(lax.div(ctx, 2), NY)
    z = lax.div(ctx, 2 * NY)
    x = xh * 2 + xl
    sister = (ctx, xh * 2 + 1 - core)
    after = lax.rem(ctx + 1, NCTX)
    before = lax.rem(ctx + NCTX - 1, NCTX)

    def at_x(d):
        other = lax.rem(x + d, NX)
        return other, (z * (2 * NY) + y * 2 + lax.rem(other, 2), lax.div(other, 2) * 2 + core)

    def at_y(d):
        other = lax.rem(y + d, NY)
        return other, (z * (2 * NY) + other * 2 + xl, head)

    def at_z(d):
        other = lax.rem(z + d, NZ)
        return other, (other * (2 * NY) + y * 2 + xl, head)

    def send(src, dst, send_sem, recv_sem, device):
        pltpu.make_async_remote_copy(
            src_ref=src, dst_ref=dst, send_sem=send_sem, recv_sem=recv_sem, device_id=device, device_id_type=MESH
        ).start()

    def local(src, dst, sem):
        pltpu.make_async_copy(src, dst, sem).start()

    def wait(ref, sem):
        pltpu.make_async_copy(ref, ref, sem).wait()

    my_rows = pl.ds(al(core, ROWS), ROWS)
    her_rows = pl.ds(al(1 - core, ROWS), ROWS)

    for g in range(GROUPS):
        for i, ref in enumerate((k_in, v_in)):
            local(
                ref.at[:, pl.ds(al(core * GROUPS + g, D), D)],
                kv.at[i, pl.ds(al(6 + core, ROWS), ROWS), pl.ds(g * D, D)],
                kv_recv.at[3, g],
            )
    for g in range(GROUPS):
        for ref, buf, sem in ((q_in, qb, q_recv), (do_in, dob, do_recv)):
            local(
                ref.at[:, pl.ds(al(core * GROUPS + g, REPEAT * D), REPEAT * D)],
                buf.at[my_rows, pl.ds(g * REPEAT * D, REPEAT * D)],
                sem.at[g],
            )

    @pl.when(xh == 0)
    def _():
        kv[:, 2 * CHIP : 3 * CHIP, :] = jnp.zeros((2, CHIP, KCOLS), BF16)

    barrier = pltpu.get_barrier_semaphore()
    partners = [sister]
    partners += [(ctx, (1 - xh) * 2 + c) for c in range(2)]
    partners += [(c, h) for c in (after, before) for h in range(4)]
    partners += [at_y(d)[1] for d in range(1, NY)] + [at_z(d)[1] for d in range(1, NZ)]
    for device in partners:
        pl.semaphore_signal(barrier, inc=1, device_id=device, device_id_type=MESH)
    pl.semaphore_wait(barrier, len(partners))

    def send_kv(g, slot, half, sem, device):
        for i, ref in enumerate((k_in, v_in)):
            send(
                ref.at[:, pl.ds(al(half * GROUPS + g, D), D)],
                kv.at[i, pl.ds(al(slot * 2 + core, ROWS), ROWS), pl.ds(g * D, D)],
                kv_send.at[sem],
                kv_recv.at[slot, g],
                device,
            )

    for g in range(GROUPS):
        send_kv(g, 3, 1 - core, 0, sister)

    for g in range(GROUPS):

        @pl.when(xh == 0)
        def _():
            for c in range(2):
                send_kv(g, 2, c, 1 + c, (ctx, 2 + c))

        for h in range(4):
            send_kv(g, xh, h % 2, 3 + h, (after, h))
        send(
            q_in.at[:, pl.ds(al((1 - core) * GROUPS + g, REPEAT * D), REPEAT * D)],
            qb.at[my_rows, pl.ds(g * REPEAT * D, REPEAT * D)],
            q_send.at[g], q_recv.at[g], sister,
        )
    for g in range(GROUPS):
        send(
            do_in.at[:, pl.ds(al((1 - core) * GROUPS + g, REPEAT * D), REPEAT * D)],
            dob.at[my_rows, pl.ds(g * REPEAT * D, REPEAT * D)],
            do_send.at[g], do_recv.at[g], sister,
        )

    for g in range(GROUPS):
        wait(kv.at[:, pl.ds(3 * CHIP, CHIP), pl.ds(g * D, D)], kv_recv.at[3, g])
    pieces = []
    for i in range(2):
        total = jnp.sum(kv[i, 3 * CHIP :, :].astype(F32), axis=0, keepdims=True)
        pieces += [total[:, g * D : (g + 1) * D] for g in range(GROUPS)]
    xs[0] = jnp.concatenate(pieces, axis=0)
    for d in range(1, NX):
        send(xs.at[0], xs.at[d], xs_send.at[d], xs_recv.at[d], at_x(d)[1])

    def summaries_along_y():
        for d in range(1, NX):
            wait(xs.at[d], xs_recv.at[d])
        mine = (xs[0] + xs[2]) / BLOCK
        others = (xs[1] + xs[3]) / BLOCK
        first = z * (2 * NY) + y * 2
        sumb[pl.ds(al(first + xl, 8), 8), :] = mine.astype(BF16).astype(F32)
        sumb[pl.ds(al(first + 1 - xl, 8), 8), :] = others.astype(BF16).astype(F32)
        rows = pl.ds(al(z * NY + y, 16), 16)
        for d in range(1, NY):
            send(sumb.at[rows, :], sumb.at[rows, :], ys_send.at[d], ys_recv.at[d], at_y(d)[1])

    def summaries_along_z():
        for d in range(1, NY):
            wait(sumb.at[pl.ds(0, 16), :], ys_recv.at[d])
        rows = pl.ds(al(z, 64), 64)
        for d in range(1, NZ):
            send(sumb.at[rows, :], sumb.at[rows, :], zs_send.at[d], zs_recv.at[d], at_z(d)[1])

    def summaries_arrived():
        for d in range(1, NZ):
            wait(sumb.at[pl.ds(0, 64), :], zs_recv.at[d])

    no_before = jnp.where(ctx == 0, LOWEST, 0.0).astype(F32)
    no_partner = jnp.where(xh == 0, LOWEST, 0.0).astype(F32)
    causal = lax.broadcasted_iota(jnp.int32, (CHIP, CHIP), 0) <= lax.broadcasted_iota(jnp.int32, (CHIP, CHIP), 1)

    def band_forward(g):
        group = pl.ds(g * D, D)
        for slot in range(2):
            wait(kv.at[:, pl.ds(slot * CHIP, CHIP), group], kv_recv.at[slot, g])

        @pl.when(xh == 1)
        def _():
            wait(kv.at[:, pl.ds(2 * CHIP, CHIP), group], kv_recv.at[2, g])

        wait(qb.at[:, pl.ds(g * REPEAT * D, REPEAT * D)], q_recv.at[g])
        for i in range(2):
            kvt[i, g] = kv[i, :, g * D : (g + 1) * D].T

        def one(j, carry):
            h = g * REPEAT + j
            q = qb[:, pl.ds(al(h, D), D)]
            s = dot_t(kv[0, :, g * D : (g + 1) * D], q)
            s_before, s_partner = s[: 2 * CHIP], s[2 * CHIP : 3 * CHIP]
            s_own = jnp.where(causal, s[3 * CHIP :], LOWEST)
            top = jnp.maximum(
                jnp.maximum(
                    jnp.max(s_before, axis=0, keepdims=True) + no_before,
                    jnp.max(s_partner, axis=0, keepdims=True) + no_partner,
                ),
                jnp.max(s_own, axis=0, keepdims=True),
            ) * LOG2
            w_before = jnp.exp2(s_before * LOG2 - (top - no_before))
            w_partner = jnp.exp2(s_partner * LOG2 - (top - no_partner))
            w_own = jnp.exp2(s_own * LOG2 - top)
            total = (
                jnp.sum(w_before, axis=0, keepdims=True)
                + jnp.sum(w_partner, axis=0, keepdims=True)
                + jnp.sum(w_own, axis=0, keepdims=True)
            )
            probs[h, : 2 * CHIP, :] = w_before.astype(BF16)
            probs[h, 2 * CHIP : 3 * CHIP, :] = w_partner.astype(BF16)
            probs[h, 3 * CHIP :, :] = w_own.astype(BF16)
            ob[h] = dot(kvt[1, g], probs[h])
            stats[h, 0:1, :] = top
            stats[h, 1:2, :] = total
            return carry

        lax.fori_loop(0, REPEAT, one, 0)

    seen = lax.broadcasted_iota(jnp.int32, (NCTX, CHIP), 0) < ctx

    def summary_part(g):
        sum_k = sumb[pl.ds(g, NCTX, stride=8), :]
        sum_v = sumb[pl.ds(GROUPS + g, NCTX, stride=8), :]
        sum_kt, sum_vt = sum_k.T.astype(BF16), sum_v.T.astype(BF16)
        sum_k, sum_v = sum_k.astype(BF16), sum_v.astype(BF16)
        wait(dob.at[:, pl.ds(g * REPEAT * D, REPEAT * D)], do_recv.at[g])

        def one(j, carry):
            grad_k, grad_v = carry
            h = g * REPEAT + j
            cols = pl.ds(al(h, D), D)
            q = qb[:, cols]
            s = jnp.where(seen, dot_t(sum_k, q), LOWEST)
            s_top = jnp.max(s, axis=0, keepdims=True) * LOG2
            w = jnp.where(seen, jnp.exp2(s * LOG2 - s_top), 0.0)
            b_top, b_total = stats[h, 0:1, :], stats[h, 1:2, :]
            top = jnp.maximum(s_top, b_top)
            b_part, s_part = jnp.exp2(b_top - top), jnp.exp2(s_top - top)
            inverse = 1.0 / (b_part * b_total + s_part * jnp.sum(w, axis=0, keepdims=True))
            b_part, s_part = b_part * inverse, s_part * inverse
            w_low = w.astype(BF16)
            attended = ob[h] * b_part + dot(sum_vt, w_low) * s_part
            outb[:, cols] = attended.T.astype(BF16)
            grad_out = dob[:, cols].astype(F32).T
            b_grad = (grad_out * (16.0 * b_part)).astype(BF16)
            s_grad = (grad_out * (16.0 * s_part)).astype(BF16)
            db[h] = b_grad
            stats[h, 2:3, :] = jnp.sum(b_grad.astype(F32) * attended, axis=0, keepdims=True)
            s_dot = jnp.sum(s_grad.astype(F32) * attended, axis=0, keepdims=True)
            slope = (w * (dot(sum_v, s_grad) - s_dot)).astype(BF16)
            gqb[h] = dot(sum_kt, slope)
            return grad_k + dot(slope, q), grad_v + dot_t(w_low, s_grad)

        zero = jnp.zeros((NCTX, D), F32)
        grad_k, grad_v = lax.fori_loop(0, REPEAT, one, (zero, zero))
        sg[pl.ds(g, NCTX, stride=8), :] = grad_k * SCALE
        sg[pl.ds(GROUPS + g, NCTX, stride=8), :] = grad_v

    def give(buf, ref, g, which):
        cols = pl.ds(g * REPEAT * D, REPEAT * D)
        out_cols = pl.ds(al(core * GROUPS + g, REPEAT * D), REPEAT * D)
        send(buf.at[her_rows, cols], ref.at[:, out_cols], o_send.at[which, g], o_recv.at[which, g], sister)
        local(buf.at[my_rows, cols], ref.at[:, out_cols], o_local.at[which, g])

    def grads_along_z():
        for d in range(1, NZ):
            other, device = at_z(d)
            send(sg.at[pl.ds(al(other, 64), 64), :], rsz.at[d], rz_send.at[d], rz_recv.at[d], device)

    def grads_along_y():
        for d in range(1, NZ):
            wait(rsz.at[d], rz_recv.at[d])
        total = sg[pl.ds(al(z, 64), 64), :]
        for d in range(1, NZ):
            total = total + rsz[d]
        acc1[...] = total
        for d in range(1, NY):
            other, device = at_y(d)
            send(acc1.at[pl.ds(al(other, 16), 16), :], rsy.at[d], ry_send.at[d], ry_recv.at[d], device)

    def grads_along_x():
        for d in range(1, NY):
            wait(rsy.at[d], ry_recv.at[d])
        total = acc1[pl.ds(al(y, 16), 16), :]
        for d in range(1, NY):
            total = total + rsy[d]
        acc2[...] = total
        for d in range(1, NX):
            other, device = at_x(d)
            send(acc2.at[pl.ds(al(lax.rem(other, 2), 8), 8), :], rsx.at[d], rx_send.at[d], rx_recv.at[d], device)

    def grads_arrived():
        for d in range(1, NX):
            wait(rsx.at[d], rx_recv.at[d])
        total = acc2[pl.ds(al(xl, 8), 8), :]
        for d in range(1, NX):
            total = total + rsx[d]
        acc3[...] = total / BLOCK

    def band_backward(g):
        def one(j, carry):
            h = g * REPEAT + j
            cols = pl.ds(al(h, D), D)
            q = qb[:, cols]
            grad = db[h]
            back = dot(kv[1, :, g * D : (g + 1) * D], grad)
            low = probs[h]
            slope = (low.astype(F32) * (back - stats[h, 2:3, :])).astype(BF16)
            grad_q = (gqb[h] + dot(kvt[0, g], slope)) * SCALE
            gqout[:, cols] = grad_q.T.astype(BF16)
            grad_k = dot(slope, q)
            grad_v = dot_t(low, grad)

            @pl.when(j == 0)
            def _():
                dkv[0] = grad_k
                dkv[1] = grad_v

            @pl.when(j > 0)
            def _():
                dkv[0] += grad_k
                dkv[1] += grad_v

            return carry

        lax.fori_loop(0, REPEAT, one, 0)
        own[0, g] = dkv[0, 3 * CHIP :, :] * SCALE
        own[1, g] = dkv[1, 3 * CHIP :, :]
        for slot in range(3):
            gsend[slot, g, 0] = (dkv[0, slot * CHIP : (slot + 1) * CHIP, :] * SCALE).astype(BF16)
            gsend[slot, g, 1] = dkv[1, slot * CHIP : (slot + 1) * CHIP, :].astype(BF16)
        for slot in range(2):
            send(
                gsend.at[slot, g], grecv.at[xh, g], g_send.at[slot, g], g_recv.at[xh, g], (before, slot * 2 + core)
            )

        @pl.when(xh == 1)
        def _():
            send(gsend.at[2, g], grecv.at[2, g], g_send.at[2, g], g_recv.at[2, g], (ctx, core))

    def finish(g):
        for slot in range(2):
            wait(grecv.at[slot, g], g_recv.at[slot, g])

        @pl.when(xh == 0)
        def _():
            wait(grecv.at[2, g], g_recv.at[2, g])
            for i in range(2):
                own[i, g] += grecv[2, g, i].astype(F32)

        for i, ref in enumerate((gk_ref, gv_ref)):
            total = own[i, g] + grecv[0, g, i].astype(F32) + grecv[1, g, i].astype(F32)
            row = i * GROUPS + g
            fin[g, i] = (total + acc3[row : row + 1, :]).astype(BF16)
            cols = pl.ds(al(core * GROUPS + g, D), D)
            send(fin.at[g, i, her_rows, :], ref.at[:, cols], f_send.at[i, g], f_recv.at[i, g], sister)
            local(fin.at[g, i, my_rows, :], ref.at[:, cols], f_local.at[i, g])

    band_forward(0)
    summaries_along_y()
    band_forward(1)
    summaries_along_z()
    band_forward(2)
    band_forward(3)
    summaries_arrived()
    for g in range(GROUPS):
        summary_part(g)
        give(outb, out_ref, g, 0)
    grads_along_z()
    band_backward(0)
    give(gqout, gq_ref, 0, 1)
    grads_along_y()
    band_backward(1)
    give(gqout, gq_ref, 1, 1)
    grads_along_x()
    band_backward(2)
    give(gqout, gq_ref, 2, 1)
    grads_arrived()
    band_backward(3)
    give(gqout, gq_ref, 3, 1)
    for g in range(GROUPS):
        finish(g)

    rows_all = kv.at[:, pl.ds(0, ROWS), :]
    wait(rows_all, kv_send.at[0])
    for h in range(4):
        wait(rows_all, kv_send.at[3 + h])

    @pl.when(xh == 0)
    def _():
        for c in range(2):
            wait(rows_all, kv_send.at[1 + c])

    @pl.when(xh == 1)
    def _():
        for g in range(GROUPS):
            wait(gsend.at[2, g], g_send.at[2, g])

    part = qb.at[my_rows, pl.ds(0, REPEAT * D)]
    for g in range(GROUPS):
        wait(part, q_send.at[g])
        wait(part, do_send.at[g])
        for slot in range(2):
            wait(gsend.at[slot, g], g_send.at[slot, g])
        for i in range(2):
            wait(part, o_send.at[i, g])
            wait(part, o_recv.at[i, g])
            wait(part, o_local.at[i, g])
            wait(fin.at[g, i, my_rows, :], f_send.at[i, g])
            wait(fin.at[g, i, my_rows, :], f_recv.at[i, g])
            wait(fin.at[g, i, my_rows, :], f_local.at[i, g])
    for d in range(1, NX):
        wait(xs.at[d], xs_send.at[d])
        wait(rsx.at[d], rx_send.at[d])
    for d in range(1, NY):
        wait(rsy.at[d], ys_send.at[d])
        wait(rsy.at[d], ry_send.at[d])
    for d in range(1, NZ):
        wait(rsz.at[d], zs_send.at[d])
        wait(rsz.at[d], rz_send.at[d])


def shards(queries, keys, values, cotangent):
    heads = GROUPS * REPEAT
    dma = pltpu.SemaphoreType.DMA
    scratch = [
        pltpu.VMEM((CHIP, QCOLS), BF16),
        pltpu.VMEM((CHIP, QCOLS), BF16),
        pltpu.VMEM((2, BAND, KCOLS), BF16),
        pltpu.VMEM((2, GROUPS, D, BAND), BF16),
        pltpu.VMEM((heads, BAND, CHIP), BF16),
        pltpu.VMEM((heads, D, CHIP), F32),
        pltpu.VMEM((heads, D, CHIP), F32),
        pltpu.VMEM((heads, D, CHIP), BF16),
        pltpu.VMEM((heads, 8, CHIP), F32),
        pltpu.VMEM((CHIP, QCOLS), BF16),
        pltpu.VMEM((CHIP, QCOLS), BF16),
        pltpu.VMEM((NX, 8, D), F32),
        pltpu.VMEM((NCTX * 8, D), F32),
        pltpu.VMEM((NCTX * 8, D), F32),
        pltpu.VMEM((NZ, 64, D), F32),
        pltpu.VMEM((NY, 16, D), F32),
        pltpu.VMEM((NX, 8, D), F32),
        pltpu.VMEM((64, D), F32),
        pltpu.VMEM((16, D), F32),
        pltpu.VMEM((8, D), F32),
        pltpu.VMEM((2, BAND, D), F32),
        pltpu.VMEM((2, GROUPS, CHIP, D), F32),
        pltpu.VMEM((3, GROUPS, 2, CHIP, D), BF16),
        pltpu.VMEM((3, GROUPS, 2, CHIP, D), BF16),
        pltpu.VMEM((GROUPS, 2, CHIP, D), BF16),
        dma((7,)), dma((4, GROUPS)),
        dma((GROUPS,)), dma((GROUPS,)), dma((GROUPS,)), dma((GROUPS,)),
        dma((NX,)), dma((NX,)), dma((NY,)), dma((NY,)), dma((NZ,)), dma((NZ,)),
        dma((NZ,)), dma((NZ,)), dma((NY,)), dma((NY,)), dma((NX,)), dma((NX,)),
        dma((3, GROUPS)), dma((3, GROUPS)),
        dma((2, GROUPS)), dma((2, GROUPS)), dma((2, GROUPS)),
        dma((2, GROUPS)), dma((2, GROUPS)), dma((2, GROUPS)),
    ]
    anywhere = pl.BlockSpec(memory_space=pl.ANY)
    return pl.pallas_call(
        kernel,
        out_shape=[jax.ShapeDtypeStruct(a.shape, BF16) for a in (queries, cotangent, keys, values)],
        in_specs=[anywhere] * 4,
        out_specs=[anywhere] * 4,
        scratch_shapes=scratch,
        compiler_params=pltpu.CompilerParams(
            collective_id=0, has_side_effects=True, vmem_limit_bytes=56 * 1024 * 1024
        ),
    )(queries, keys, values, cotangent)


def solution(mesh):
    placed = P(("ctx", "head"), None)
    return jax.shard_map(
        shards, mesh=mesh, in_specs=(placed,) * 4, out_specs=(placed,) * 4, check_vma=False
    )
```

```python
import math

import jax
import jax.numpy as jnp
from jax import lax
from jax.experimental import pallas as pl
from jax.experimental.pallas import tpu as pltpu
from jax.sharding import PartitionSpec as P

MESH = pl.DeviceIdType.MESH
F32 = jnp.float32
BF16 = jnp.bfloat16

D = 128
BLOCK = 512
ROWS = 128
CHIP = 256
GROUPS = 4
REPEAT = 4
KCOLS = GROUPS * D
QCOLS = GROUPS * REPEAT * D
BAND = 4 * CHIP
NX, NY, NZ = 4, 4, 8
NCTX = 64
LOWEST = -1e30
SCALE = 1.0 / math.sqrt(D)
LOG2 = SCALE / math.log(2.0)


def dot(a, b):
    return jnp.dot(a, b, preferred_element_type=F32)


def dot_t(a, b):
    return lax.dot_general(a, b, (((1,), (1,)), ((), ())), preferred_element_type=F32)


def al(index, size):
    return pl.multiple_of(index * size, size)


def kernel(
    q_in, k_in, v_in, do_in, out_ref, gq_ref, gk_ref, gv_ref,
    qb, dob, kv, kvt, probs, slopes, ob, gqb, db, stats, outb, gqout,
    xs, sumb, sg, rsz, rsy, rsx, acc1, acc2, acc3,
    dkv, own, gsend, grecv, fin,
    kv_send, kv_recv, q_send, do_send, q_recv, do_recv,
    xs_send, xs_recv, ys_send, ys_recv, zs_send, zs_recv,
    rz_send, rz_recv, ry_send, ry_recv, rx_send, rx_recv,
    g_send, g_recv, o_send, o_recv, o_local, f_send, f_recv, f_local,
):
    ctx = lax.axis_index("ctx")
    head = lax.axis_index("head")
    core = lax.rem(head, 2)
    xh = lax.div(head, 2)
    xl = lax.rem(ctx, 2)
    y = lax.rem(lax.div(ctx, 2), NY)
    z = lax.div(ctx, 2 * NY)
    x = xh * 2 + xl
    sister = (ctx, xh * 2 + 1 - core)
    after = lax.rem(ctx + 1, NCTX)
    before = lax.rem(ctx + NCTX - 1, NCTX)

    def at_x(d):
        other = lax.rem(x + d, NX)
        return other, (z * (2 * NY) + y * 2 + lax.rem(other, 2), lax.div(other, 2) * 2 + core)

    def at_y(d):
        other = lax.rem(y + d, NY)
        return other, (z * (2 * NY) + other * 2 + xl, head)

    def at_z(d):
        other = lax.rem(z + d, NZ)
        return other, (other * (2 * NY) + y * 2 + xl, head)

    def send(src, dst, send_sem, recv_sem, device):
        pltpu.make_async_remote_copy(
            src_ref=src, dst_ref=dst, send_sem=send_sem, recv_sem=recv_sem, device_id=device, device_id_type=MESH
        ).start()

    def local(src, dst, sem):
        pltpu.make_async_copy(src, dst, sem).start()

    def wait(ref, sem):
        pltpu.make_async_copy(ref, ref, sem).wait()

    my_rows = pl.ds(al(core, ROWS), ROWS)
    her_rows = pl.ds(al(1 - core, ROWS), ROWS)

    for g in range(GROUPS):
        for i, ref in enumerate((k_in, v_in)):
            local(
                ref.at[:, pl.ds(al(core * GROUPS + g, D), D)],
                kv.at[i, pl.ds(al(6 + core, ROWS), ROWS), pl.ds(g * D, D)],
                kv_recv.at[3, g],
            )
    for g in range(GROUPS):
        for ref, buf, sem in ((q_in, qb, q_recv), (do_in, dob, do_recv)):
            local(
                ref.at[:, pl.ds(al(core * GROUPS + g, REPEAT * D), REPEAT * D)],
                buf.at[my_rows, pl.ds(g * REPEAT * D, REPEAT * D)],
                sem.at[g],
            )

    @pl.when(xh == 0)
    def _():
        kv[:, 2 * CHIP : 3 * CHIP, :] = jnp.zeros((2, CHIP, KCOLS), BF16)

    barrier = pltpu.get_barrier_semaphore()
    partners = [sister]
    partners += [(ctx, (1 - xh) * 2 + c) for c in range(2)]
    partners += [(c, h) for c in (after, before) for h in range(4)]
    partners += [at_y(d)[1] for d in range(1, NY)] + [at_z(d)[1] for d in range(1, NZ)]
    for device in partners:
        pl.semaphore_signal(barrier, inc=1, device_id=device, device_id_type=MESH)
    pl.semaphore_wait(barrier, len(partners))

    def send_kv(g, slot, half, sem, device):
        for i, ref in enumerate((k_in, v_in)):
            send(
                ref.at[:, pl.ds(al(half * GROUPS + g, D), D)],
                kv.at[i, pl.ds(al(slot * 2 + core, ROWS), ROWS), pl.ds(al(g, D), D)],
                kv_send.at[sem],
                kv_recv.at[slot, g],
                device,
            )

    def send_group(g):
        @pl.when(xh == 0)
        def _():
            for c in range(2):
                send_kv(g, 2, c, 1 + c, (ctx, 2 + c))

        for h in range(4):
            send_kv(g, xh, h % 2, 3 + h, (after, h))

    for g in range(GROUPS):
        send_kv(g, 3, 1 - core, 0, sister)
    send_group(0)
    for ref, buf, send_sem, recv_sem in ((q_in, qb, q_send, q_recv), (do_in, dob, do_send, do_recv)):
        for g in range(GROUPS):
            send(
                ref.at[:, pl.ds(al((1 - core) * GROUPS + g, REPEAT * D), REPEAT * D)],
                buf.at[my_rows, pl.ds(g * REPEAT * D, REPEAT * D)],
                send_sem.at[g], recv_sem.at[g], sister,
            )
    send_group(1)

    for g in range(GROUPS):
        wait(kv.at[:, pl.ds(3 * CHIP, CHIP), pl.ds(g * D, D)], kv_recv.at[3, g])
    pieces = []
    for i in range(2):
        total = jnp.sum(kv[i, 3 * CHIP :, :].astype(F32), axis=0, keepdims=True)
        pieces += [total[:, g * D : (g + 1) * D] for g in range(GROUPS)]
    xs[0] = jnp.concatenate(pieces, axis=0)
    for d in range(1, NX):
        send(xs.at[0], xs.at[d], xs_send.at[d], xs_recv.at[d], at_x(d)[1])

    def summaries_along_y():
        for d in range(1, NX):
            wait(xs.at[d], xs_recv.at[d])
        mine = (xs[0] + xs[2]) / BLOCK
        others = (xs[1] + xs[3]) / BLOCK
        first = z * (2 * NY) + y * 2
        sumb[pl.ds(al(first + xl, 8), 8), :] = mine.astype(BF16).astype(F32)
        sumb[pl.ds(al(first + 1 - xl, 8), 8), :] = others.astype(BF16).astype(F32)
        rows = pl.ds(al(z * NY + y, 16), 16)
        for d in range(1, NY):
            send(sumb.at[rows, :], sumb.at[rows, :], ys_send.at[d], ys_recv.at[d], at_y(d)[1])

    def summaries_along_z():
        for d in range(1, NY):
            wait(sumb.at[pl.ds(0, 16), :], ys_recv.at[d])
        rows = pl.ds(al(z, 64), 64)
        for d in range(1, NZ):
            send(sumb.at[rows, :], sumb.at[rows, :], zs_send.at[d], zs_recv.at[d], at_z(d)[1])

    def summaries_arrived():
        for d in range(1, NZ):
            wait(sumb.at[pl.ds(0, 64), :], zs_recv.at[d])

    no_before = jnp.where(ctx == 0, LOWEST, 0.0).astype(F32)
    no_partner = jnp.where(xh == 0, LOWEST, 0.0).astype(F32)
    causal = lax.broadcasted_iota(jnp.int32, (CHIP, CHIP), 0) <= lax.broadcasted_iota(jnp.int32, (CHIP, CHIP), 1)

    def band_forward(g):
        group = pl.ds(al(g, D), D)
        for slot in range(2):
            wait(kv.at[:, pl.ds(slot * CHIP, CHIP), group], kv_recv.at[slot, g])

        @pl.when(xh == 1)
        def _():
            wait(kv.at[:, pl.ds(2 * CHIP, CHIP), group], kv_recv.at[2, g])

        wait(qb.at[:, pl.ds(al(g, REPEAT * D), REPEAT * D)], q_recv.at[g])

        @pl.when(g + 2 < GROUPS)
        def _():
            send_group(g + 2)

        for i in range(2):
            kvt[i, g] = kv[i, :, group].T

        for j in range(REPEAT):
            columns = slice(j * CHIP, (j + 1) * CHIP)
            q = qb[:, pl.ds(al(g * REPEAT + j, D), D)]
            s = dot_t(kv[0, :, group], q)
            s_before, s_partner = s[: 2 * CHIP], s[2 * CHIP : 3 * CHIP]
            s_own = jnp.where(causal, s[3 * CHIP :], LOWEST)
            top = jnp.maximum(
                jnp.maximum(
                    jnp.max(s_before, axis=0, keepdims=True) + no_before,
                    jnp.max(s_partner, axis=0, keepdims=True) + no_partner,
                ),
                jnp.max(s_own, axis=0, keepdims=True),
            ) * LOG2
            w_before = jnp.exp2(s_before * LOG2 - (top - no_before))
            w_partner = jnp.exp2(s_partner * LOG2 - (top - no_partner))
            w_own = jnp.exp2(s_own * LOG2 - top)
            total = (
                jnp.sum(w_before, axis=0, keepdims=True)
                + jnp.sum(w_partner, axis=0, keepdims=True)
                + jnp.sum(w_own, axis=0, keepdims=True)
            )
            low = jnp.concatenate([w.astype(BF16) for w in (w_before, w_partner, w_own)], axis=0)
            probs[g, :, columns] = low
            ob[g, :, columns] = dot(kvt[1, g], low)
            stats[g, 0:1, columns] = top
            stats[g, 1:2, columns] = total

    seen = lax.broadcasted_iota(jnp.int32, (NCTX, REPEAT * CHIP), 0) < ctx

    def stacked_queries(g):
        return jnp.concatenate([qb[:, pl.ds(al(g * REPEAT + j, D), D)] for j in range(REPEAT)], axis=0)

    def summary_part(g):
        sum_k = sumb[pl.ds(g, NCTX, stride=8), :]
        sum_v = sumb[pl.ds(GROUPS + g, NCTX, stride=8), :]
        sum_kt, sum_vt = sum_k.T.astype(BF16), sum_v.T.astype(BF16)
        sum_k, sum_v = sum_k.astype(BF16), sum_v.astype(BF16)
        wait(dob.at[:, pl.ds(al(g, REPEAT * D), REPEAT * D)], do_recv.at[g])
        q = stacked_queries(g)
        s = jnp.where(seen, dot_t(sum_k, q), LOWEST)
        s_top = jnp.max(s, axis=0, keepdims=True) * LOG2
        w = jnp.where(seen, jnp.exp2(s * LOG2 - s_top), 0.0)
        b_top, b_total = stats[g, 0:1, :], stats[g, 1:2, :]
        top = jnp.maximum(s_top, b_top)
        b_part, s_part = jnp.exp2(b_top - top), jnp.exp2(s_top - top)
        inverse = 1.0 / (b_part * b_total + s_part * jnp.sum(w, axis=0, keepdims=True))
        b_part, s_part = b_part * inverse, s_part * inverse
        w_low = w.astype(BF16)
        attended = ob[g] * b_part + dot(sum_vt, w_low) * s_part
        grads = []
        for j in range(REPEAT):
            cols = pl.ds(al(g * REPEAT + j, D), D)
            outb[:, cols] = attended[:, j * CHIP : (j + 1) * CHIP].T.astype(BF16)
            grads.append(dob[:, cols].astype(F32).T)
        grad_out = jnp.concatenate(grads, axis=1)
        b_grad = (grad_out * (16.0 * b_part)).astype(BF16)
        s_grad = (grad_out * (16.0 * s_part)).astype(BF16)
        db[g] = b_grad
        stats[g, 2:3, :] = jnp.sum(b_grad.astype(F32) * attended, axis=0, keepdims=True)
        s_dot = jnp.sum(s_grad.astype(F32) * attended, axis=0, keepdims=True)
        slope = (w * (dot(sum_v, s_grad) - s_dot)).astype(BF16)
        gqb[g] = dot(sum_kt, slope)
        sg[pl.ds(g, NCTX, stride=8), :] = dot(slope, q) * SCALE
        sg[pl.ds(GROUPS + g, NCTX, stride=8), :] = dot_t(w_low, s_grad)
        give(outb, out_ref, g, 0)

    def give(buf, ref, g, which):
        cols = pl.ds(al(g, REPEAT * D), REPEAT * D)
        out_cols = pl.ds(al(core * GROUPS + g, REPEAT * D), REPEAT * D)
        send(buf.at[her_rows, cols], ref.at[:, out_cols], o_send.at[which, g], o_recv.at[which, g], sister)
        local(buf.at[my_rows, cols], ref.at[:, out_cols], o_local.at[which, g])

    def grads_along_z():
        for d in range(1, NZ):
            other, device = at_z(d)
            send(sg.at[pl.ds(al(other, 64), 64), :], rsz.at[d], rz_send.at[d], rz_recv.at[d], device)

    def grads_along_y():
        for d in range(1, NZ):
            wait(rsz.at[d], rz_recv.at[d])
        total = sg[pl.ds(al(z, 64), 64), :]
        for d in range(1, NZ):
            total = total + rsz[d]
        acc1[...] = total
        for d in range(1, NY):
            other, device = at_y(d)
            send(acc1.at[pl.ds(al(other, 16), 16), :], rsy.at[d], ry_send.at[d], ry_recv.at[d], device)

    def grads_along_x():
        for d in range(1, NY):
            wait(rsy.at[d], ry_recv.at[d])
        total = acc1[pl.ds(al(y, 16), 16), :]
        for d in range(1, NY):
            total = total + rsy[d]
        acc2[...] = total
        for d in range(1, NX):
            other, device = at_x(d)
            send(acc2.at[pl.ds(al(lax.rem(other, 2), 8), 8), :], rsx.at[d], rx_send.at[d], rx_recv.at[d], device)

    def grads_arrived():
        for d in range(1, NX):
            wait(rsx.at[d], rx_recv.at[d])
        total = acc2[pl.ds(al(xl, 8), 8), :]
        for d in range(1, NX):
            total = total + rsx[d]
        acc3[...] = total / BLOCK

    def band_backward(g):
        group = pl.ds(al(g, D), D)
        for j in range(REPEAT):
            columns = slice(j * CHIP, (j + 1) * CHIP)
            back = dot(kv[1, :, group], db[g, :, columns])
            slope = (probs[g, :, columns].astype(F32) * (back - stats[g, 2:3, columns])).astype(BF16)
            slopes[:, columns] = slope
            grad_q = (gqb[g, :, columns] + dot(kvt[0, g], slope)) * SCALE
            gqout[:, pl.ds(al(g * REPEAT + j, D), D)] = grad_q.T.astype(BF16)
        give(gqout, gq_ref, g, 1)
        dkv[0] = dot(slopes[...], stacked_queries(g))
        dkv[1] = dot_t(probs[g], db[g])
        own[0, g] = dkv[0, 3 * CHIP :, :] * SCALE
        own[1, g] = dkv[1, 3 * CHIP :, :]
        for slot in range(3):
            gsend[slot, g, 0] = (dkv[0, slot * CHIP : (slot + 1) * CHIP, :] * SCALE).astype(BF16)
            gsend[slot, g, 1] = dkv[1, slot * CHIP : (slot + 1) * CHIP, :].astype(BF16)
        for slot in range(2):
            send(
                gsend.at[slot, g], grecv.at[xh, g], g_send.at[slot, g], g_recv.at[xh, g], (before, slot * 2 + core)
            )

        @pl.when(xh == 1)
        def _():
            send(gsend.at[2, g], grecv.at[2, g], g_send.at[2, g], g_recv.at[2, g], (ctx, core))

    def finish(g):
        for slot in range(2):
            wait(grecv.at[slot, g], g_recv.at[slot, g])

        @pl.when(xh == 0)
        def _():
            wait(grecv.at[2, g], g_recv.at[2, g])
            for i in range(2):
                own[i, g] += grecv[2, g, i].astype(F32)

        for i, ref in enumerate((gk_ref, gv_ref)):
            total = own[i, g] + grecv[0, g, i].astype(F32) + grecv[1, g, i].astype(F32)
            row = i * GROUPS + g
            fin[g, i] = (total + acc3[row : row + 1, :]).astype(BF16)
            cols = pl.ds(al(core * GROUPS + g, D), D)
            send(fin.at[g, i, her_rows, :], ref.at[:, cols], f_send.at[i, g], f_recv.at[i, g], sister)
            local(fin.at[g, i, my_rows, :], ref.at[:, cols], f_local.at[i, g])

    summaries_along_y()

    def step(t, carry):
        @pl.when(t < GROUPS)
        def _():
            band_forward(t)

        @pl.when(t == 0)
        def _():
            summaries_along_z()

        @pl.when(t == 1)
        def _():
            summaries_arrived()

        @pl.when((t > 0) & (t < GROUPS))
        def _():
            def part(g, carry):
                summary_part(g)
                return carry

            lax.fori_loop(jnp.where(t == 1, 0, t), t + 1, part, 0)

        @pl.when(t == GROUPS - 1)
        def _():
            grads_along_z()

        @pl.when(t == GROUPS)
        def _():
            grads_along_y()

        @pl.when(t > 0)
        def _():
            band_backward(t - 1)

        return carry

    lax.fori_loop(0, GROUPS + 1, step, 0)
    grads_along_x()
    grads_arrived()
    for g in range(GROUPS):
        finish(g)

    rows_all = kv.at[:, pl.ds(0, ROWS), :]
    wait(rows_all, kv_send.at[0])
    for h in range(4):
        wait(rows_all, kv_send.at[3 + h])

    @pl.when(xh == 0)
    def _():
        for c in range(2):
            wait(rows_all, kv_send.at[1 + c])

    @pl.when(xh == 1)
    def _():
        for g in range(GROUPS):
            wait(gsend.at[2, g], g_send.at[2, g])

    part = qb.at[my_rows, pl.ds(0, REPEAT * D)]
    for g in range(GROUPS):
        wait(part, q_send.at[g])
        wait(part, do_send.at[g])
        for slot in range(2):
            wait(gsend.at[slot, g], g_send.at[slot, g])
        for i in range(2):
            wait(part, o_send.at[i, g])
            wait(part, o_recv.at[i, g])
            wait(part, o_local.at[i, g])
            wait(fin.at[g, i, my_rows, :], f_send.at[i, g])
            wait(fin.at[g, i, my_rows, :], f_recv.at[i, g])
            wait(fin.at[g, i, my_rows, :], f_local.at[i, g])
    for d in range(1, NX):
        wait(xs.at[d], xs_send.at[d])
        wait(rsx.at[d], rx_send.at[d])
    for d in range(1, NY):
        wait(rsy.at[d], ys_send.at[d])
        wait(rsy.at[d], ry_send.at[d])
    for d in range(1, NZ):
        wait(rsz.at[d], zs_send.at[d])
        wait(rsz.at[d], rz_send.at[d])


def shards(queries, keys, values, cotangent):
    dma = pltpu.SemaphoreType.DMA
    scratch = [
        pltpu.VMEM((CHIP, QCOLS), BF16),
        pltpu.VMEM((CHIP, QCOLS), BF16),
        pltpu.VMEM((2, BAND, KCOLS), BF16),
        pltpu.VMEM((2, GROUPS, D, BAND), BF16),
        pltpu.VMEM((GROUPS, BAND, REPEAT * CHIP), BF16),
        pltpu.VMEM((BAND, REPEAT * CHIP), BF16),
        pltpu.VMEM((GROUPS, D, REPEAT * CHIP), F32),
        pltpu.VMEM((GROUPS, D, REPEAT * CHIP), F32),
        pltpu.VMEM((GROUPS, D, REPEAT * CHIP), BF16),
        pltpu.VMEM((GROUPS, 8, REPEAT * CHIP), F32),
        pltpu.VMEM((CHIP, QCOLS), BF16),
        pltpu.VMEM((CHIP, QCOLS), BF16),
        pltpu.VMEM((NX, 8, D), F32),
        pltpu.VMEM((NCTX * 8, D), F32),
        pltpu.VMEM((NCTX * 8, D), F32),
        pltpu.VMEM((NZ, 64, D), F32),
        pltpu.VMEM((NY, 16, D), F32),
        pltpu.VMEM((NX, 8, D), F32),
        pltpu.VMEM((64, D), F32),
        pltpu.VMEM((16, D), F32),
        pltpu.VMEM((8, D), F32),
        pltpu.VMEM((2, BAND, D), F32),
        pltpu.VMEM((2, GROUPS, CHIP, D), F32),
        pltpu.VMEM((3, GROUPS, 2, CHIP, D), BF16),
        pltpu.VMEM((3, GROUPS, 2, CHIP, D), BF16),
        pltpu.VMEM((GROUPS, 2, CHIP, D), BF16),
        dma((7,)), dma((4, GROUPS)),
        dma((GROUPS,)), dma((GROUPS,)), dma((GROUPS,)), dma((GROUPS,)),
        dma((NX,)), dma((NX,)), dma((NY,)), dma((NY,)), dma((NZ,)), dma((NZ,)),
        dma((NZ,)), dma((NZ,)), dma((NY,)), dma((NY,)), dma((NX,)), dma((NX,)),
        dma((3, GROUPS)), dma((3, GROUPS)),
        dma((2, GROUPS)), dma((2, GROUPS)), dma((2, GROUPS)),
        dma((2, GROUPS)), dma((2, GROUPS)), dma((2, GROUPS)),
    ]
    anywhere = pl.BlockSpec(memory_space=pl.ANY)
    return pl.pallas_call(
        kernel,
        out_shape=[jax.ShapeDtypeStruct(a.shape, BF16) for a in (queries, cotangent, keys, values)],
        in_specs=[anywhere] * 4,
        out_specs=[anywhere] * 4,
        scratch_shapes=scratch,
        compiler_params=pltpu.CompilerParams(
            collective_id=0, has_side_effects=True, vmem_limit_bytes=56 * 1024 * 1024
        ),
    )(queries, keys, values, cotangent)


def solution(mesh):
    placed = P(("ctx", "head"), None)
    return jax.shard_map(
        shards, mesh=mesh, in_specs=(placed,) * 4, out_specs=(placed,) * 4, check_vma=False
    )
```

```python
import math

import jax
import jax.numpy as jnp
from jax import lax
from jax.experimental import pallas as pl
from jax.experimental.pallas import tpu as pltpu
from jax.sharding import PartitionSpec as P

MESH = pl.DeviceIdType.MESH
F32 = jnp.float32
BF16 = jnp.bfloat16

D = 128
BLOCK = 512
ROWS = 128
CHIP = 256
GROUPS = 4
REPEAT = 4
KCOLS = GROUPS * D
QCOLS = GROUPS * REPEAT * D
BAND = 4 * CHIP
NX, NY, NZ = 4, 4, 8
NCTX = 64
LOWEST = -1e30
SCALE = 1.0 / math.sqrt(D)
LOG2 = SCALE / math.log(2.0)


def dot(a, b):
    return jnp.dot(a, b, preferred_element_type=F32)


def dot_t(a, b):
    return lax.dot_general(a, b, (((1,), (1,)), ((), ())), preferred_element_type=F32)


def al(index, size):
    return pl.multiple_of(index * size, size)


def kernel(
    q_in, k_in, v_in, do_in, out_ref, gq_ref, gk_ref, gv_ref,
    qb, dob, kv, kvt, probs, slopes, ob, gqb, db, stats, outb, gqout,
    kvl, stage, sums, xs, sumb, sg, rsz, rsy, rsx, acc1, acc2, acc3,
    own, gsend, grecv, fin,
    l_sem, st_send, st_recv, kv_send, kv_recv, own_recv, q_send, do_send, q_recv, do_recv,
    xs_send, xs_recv, ys_send, ys_recv, zs_send, zs_recv,
    rz_send, rz_recv, ry_send, ry_recv, rx_send, rx_recv,
    g_send, g_recv, o_send, o_recv, o_local, f_send, f_recv, f_local,
):
    ctx = lax.axis_index("ctx")
    head = lax.axis_index("head")
    core = lax.rem(head, 2)
    xh = lax.div(head, 2)
    xl = lax.rem(ctx, 2)
    y = lax.rem(lax.div(ctx, 2), NY)
    z = lax.div(ctx, 2 * NY)
    x = xh * 2 + xl
    sister = (ctx, xh * 2 + 1 - core)
    after = lax.rem(ctx + 1, NCTX)
    before = lax.rem(ctx + NCTX - 1, NCTX)
    onward = lax.rem(ctx + 2, NCTX)
    behind = lax.rem(ctx + NCTX - 2, NCTX)

    def at_x(d):
        other = lax.rem(x + d, NX)
        return other, (z * (2 * NY) + y * 2 + lax.rem(other, 2), lax.div(other, 2) * 2 + core)

    def at_y(d):
        other = lax.rem(y + d, NY)
        return other, (z * (2 * NY) + other * 2 + xl, head)

    def at_z(d):
        other = lax.rem(z + d, NZ)
        return other, (other * (2 * NY) + y * 2 + xl, head)

    def send(src, dst, send_sem, recv_sem, device):
        pltpu.make_async_remote_copy(
            src_ref=src, dst_ref=dst, send_sem=send_sem, recv_sem=recv_sem, device_id=device, device_id_type=MESH
        ).start()

    def local(src, dst, sem):
        pltpu.make_async_copy(src, dst, sem).start()

    def wait(ref, sem):
        pltpu.make_async_copy(ref, ref, sem).wait()

    my_rows = pl.ds(al(core, ROWS), ROWS)
    her_rows = pl.ds(al(1 - core, ROWS), ROWS)

    barrier = pltpu.get_barrier_semaphore()
    partners = [sister]
    partners += [(ctx, (1 - xh) * 2 + c) for c in range(2)]
    partners += [(c, h) for c in (after, before) for h in range(4)]
    partners += [(onward, head), (behind, head)]
    partners += [at_y(d)[1] for d in range(1, NY)] + [at_z(d)[1] for d in range(1, NZ)]
    for device in partners:
        pl.semaphore_signal(barrier, inc=1, device_id=device, device_id_type=MESH)

    for i, ref in enumerate((k_in, v_in)):
        local(ref, kvl.at[i], l_sem.at[i])

    for i, ref in enumerate((k_in, v_in)):
        local(ref.at[:, pl.ds(al(core, KCOLS), KCOLS)], kv.at[i, pl.ds(al(6 + core, ROWS), ROWS), :], own_recv)
    for ref, buf, sem in ((q_in, qb, q_recv), (do_in, dob, do_recv)):
        local(ref.at[:, pl.ds(al(core, QCOLS), QCOLS)], buf.at[my_rows, :], sem)

    @pl.when(xh == 0)
    def _():
        kv[:, 2 * CHIP : 3 * CHIP, :] = jnp.zeros((2, CHIP, KCOLS), BF16)

    pieces = ([], [])
    for i in range(2):
        wait(kvl.at[i], l_sem.at[i])
        total = jnp.sum(kvl[i].astype(F32), axis=0, keepdims=True)
        for half in range(2):
            pieces[half].extend(total[:, (half * GROUPS + g) * D : (half * GROUPS + g + 1) * D] for g in range(GROUPS))
    for half in range(2):
        sums[half] = jnp.concatenate(pieces[half], axis=0)
    xs[0] = sums[core]
    pl.semaphore_wait(barrier, len(partners))
    for d in range(NX):
        for other in range(2):
            if d + other > 0:
                half = 1 - core if other else core
                ctx_x, head_x = at_x(d)[1]
                slot = 2 * d + other
                device = (ctx_x, head_x - core + half)
                send(sums.at[half], xs.at[slot], xs_send.at[slot], xs_recv.at[slot], device)

    def send_kv(src, g, slot, half, sem, device):
        send(
            src.at[:, :, pl.ds(al(half * GROUPS + g, D), D)],
            kv.at[:, pl.ds(al(slot * 2 + core, ROWS), ROWS), pl.ds(al(g, D), D)],
            kv_send.at[sem],
            kv_recv.at[slot, g],
            device,
        )

    def send_ahead(g):
        @pl.when(xl == 1)
        def _():
            for half in range(2):
                cols = pl.ds(al(half * GROUPS + g, D), D)
                send(kvl.at[:, :, cols], stage.at[:, :, cols], st_send, st_recv.at[g], (onward, head))

    def send_group(g):
        @pl.when(xl == 0)
        def _():
            for h in range(4):
                send_kv(kvl, g, xh, h % 2, 3 + h, (after, h))

        @pl.when(xh == 0)
        def _():
            for c in range(2):
                send_kv(kvl, g, 2, c, 1 + c, (ctx, 2 + c))

    def pass_on(g):
        @pl.when(xl == 1)
        def _():
            wait(stage.at[:, :, pl.ds(0, 2 * D)], st_recv.at[g])
            for h in range(4):
                send_kv(stage, g, xh, h % 2, 3 + h, (before, h))

    def exchange_cores():
        send(
            kvl.at[:, :, pl.ds(al(1 - core, KCOLS), KCOLS)],
            kv.at[:, pl.ds(al(6 + core, ROWS), ROWS), :],
            kv_send.at[0], own_recv, sister,
        )
        her_cols = pl.ds(al(1 - core, QCOLS), QCOLS)
        send(q_in.at[:, her_cols], qb.at[my_rows, :], q_send, q_recv, sister)
        send(do_in.at[:, her_cols], dob.at[my_rows, :], do_send, do_recv, sister)

    def summaries_along_y():
        for slot in range(1, 2 * NX):
            wait(xs.at[slot], xs_recv.at[slot])
        mine = (xs[0] + xs[1] + xs[4] + xs[5]) / BLOCK
        others = (xs[2] + xs[3] + xs[6] + xs[7]) / BLOCK
        first = z * (2 * NY) + y * 2
        sumb[pl.ds(al(first + xl, 8), 8), :] = mine.astype(BF16).astype(F32)
        sumb[pl.ds(al(first + 1 - xl, 8), 8), :] = others.astype(BF16).astype(F32)
        rows = pl.ds(al(z * NY + y, 16), 16)
        for d in range(1, NY):
            send(sumb.at[rows, :], sumb.at[rows, :], ys_send.at[d], ys_recv.at[d], at_y(d)[1])

    def summaries_along_z():
        for d in range(1, NY):
            wait(sumb.at[pl.ds(0, 16), :], ys_recv.at[d])
        rows = pl.ds(al(z, 64), 64)
        for d in range(1, NZ):
            send(sumb.at[rows, :], sumb.at[rows, :], zs_send.at[d], zs_recv.at[d], at_z(d)[1])

    def summaries_arrived():
        for d in range(1, NZ):
            wait(sumb.at[pl.ds(0, 64), :], zs_recv.at[d])

    no_before = jnp.where(ctx == 0, LOWEST, 0.0).astype(F32)
    no_partner = jnp.where(xh == 0, LOWEST, 0.0).astype(F32)
    causal = lax.broadcasted_iota(jnp.int32, (CHIP, CHIP), 0) <= lax.broadcasted_iota(jnp.int32, (CHIP, CHIP), 1)

    def band_forward(g):
        group = pl.ds(al(g, D), D)
        @pl.when(g == 0)
        def _():
            wait(kv.at[:, pl.ds(3 * CHIP, CHIP), :], own_recv)
            wait(qb, q_recv)

        for slot in range(2):
            wait(kv.at[:, pl.ds(slot * CHIP, CHIP), group], kv_recv.at[slot, g])

        @pl.when(xh == 1)
        def _():
            wait(kv.at[:, pl.ds(2 * CHIP, CHIP), group], kv_recv.at[2, g])

        @pl.when(g + 1 < GROUPS)
        def _():
            send_group(g + 1)
            pass_on(g + 1)

        @pl.when(g + 2 < GROUPS)
        def _():
            send_ahead(g + 2)

        for i in range(2):
            kvt[i, g] = kv[i, :, group].T

        for j in range(REPEAT):
            columns = slice(j * CHIP, (j + 1) * CHIP)
            q = qb[:, pl.ds(al(g * REPEAT + j, D), D)]
            s = dot_t(kv[0, :, group], q)
            s_before, s_partner = s[: 2 * CHIP], s[2 * CHIP : 3 * CHIP]
            s_own = jnp.where(causal, s[3 * CHIP :], LOWEST)
            top = jnp.maximum(
                jnp.maximum(
                    jnp.max(s_before, axis=0, keepdims=True) + no_before,
                    jnp.max(s_partner, axis=0, keepdims=True) + no_partner,
                ),
                jnp.max(s_own, axis=0, keepdims=True),
            ) * LOG2
            w_before = jnp.exp2(s_before * LOG2 - (top - no_before))
            w_partner = jnp.exp2(s_partner * LOG2 - (top - no_partner))
            w_own = jnp.exp2(s_own * LOG2 - top)
            total = (
                jnp.sum(w_before, axis=0, keepdims=True)
                + jnp.sum(w_partner, axis=0, keepdims=True)
                + jnp.sum(w_own, axis=0, keepdims=True)
            )
            low = jnp.concatenate([w.astype(BF16) for w in (w_before, w_partner, w_own)], axis=0)
            probs[g, :, columns] = low
            ob[g, :, columns] = dot(kvt[1, g], low)
            stats[g, 0:1, columns] = top
            stats[g, 1:2, columns] = total

    seen = lax.broadcasted_iota(jnp.int32, (NCTX, REPEAT * CHIP), 0) < ctx

    def stacked_queries(g):
        return jnp.concatenate([qb[:, pl.ds(al(g * REPEAT + j, D), D)] for j in range(REPEAT)], axis=0)

    def summary_part(g):
        sum_k = sumb[pl.ds(g, NCTX, stride=8), :]
        sum_v = sumb[pl.ds(GROUPS + g, NCTX, stride=8), :]
        sum_kt, sum_vt = sum_k.T.astype(BF16), sum_v.T.astype(BF16)
        sum_k, sum_v = sum_k.astype(BF16), sum_v.astype(BF16)
        q = stacked_queries(g)
        s = jnp.where(seen, dot_t(sum_k, q), LOWEST)
        s_top = jnp.max(s, axis=0, keepdims=True) * LOG2
        w = jnp.where(seen, jnp.exp2(s * LOG2 - s_top), 0.0)
        b_top, b_total = stats[g, 0:1, :], stats[g, 1:2, :]
        top = jnp.maximum(s_top, b_top)
        b_part, s_part = jnp.exp2(b_top - top), jnp.exp2(s_top - top)
        inverse = 1.0 / (b_part * b_total + s_part * jnp.sum(w, axis=0, keepdims=True))
        b_part, s_part = b_part * inverse, s_part * inverse
        w_low = w.astype(BF16)
        attended = ob[g] * b_part + dot(sum_vt, w_low) * s_part
        grads = []
        for j in range(REPEAT):
            cols = pl.ds(al(g * REPEAT + j, D), D)
            outb[:, cols] = attended[:, j * CHIP : (j + 1) * CHIP].T.astype(BF16)
            grads.append(dob[:, cols].astype(F32).T)
        grad_out = jnp.concatenate(grads, axis=1)
        b_grad = (grad_out * (16.0 * b_part)).astype(BF16)
        s_grad = (grad_out * (16.0 * s_part)).astype(BF16)
        db[g] = b_grad
        stats[g, 2:3, :] = jnp.sum(b_grad.astype(F32) * attended, axis=0, keepdims=True)
        s_dot = jnp.sum(s_grad.astype(F32) * attended, axis=0, keepdims=True)
        slope = (w * (dot(sum_v, s_grad) - s_dot)).astype(BF16)
        gqb[g] = dot(sum_kt, slope)
        sg[pl.ds(g, NCTX, stride=8), :] = dot(slope, q) * SCALE
        sg[pl.ds(GROUPS + g, NCTX, stride=8), :] = dot_t(w_low, s_grad)
        give(outb, out_ref, g, 0)

    def give(buf, ref, g, which):
        cols = pl.ds(al(g, REPEAT * D), REPEAT * D)
        out_cols = pl.ds(al(core * GROUPS + g, REPEAT * D), REPEAT * D)
        send(buf.at[her_rows, cols], ref.at[:, out_cols], o_send.at[which, g], o_recv.at[which, g], sister)
        local(buf.at[my_rows, cols], ref.at[:, out_cols], o_local.at[which, g])

    def grads_along_z():
        for d in range(1, NZ):
            other, device = at_z(d)
            send(sg.at[pl.ds(al(other, 64), 64), :], rsz.at[d], rz_send.at[d], rz_recv.at[d], device)

    def grads_along_y():
        for d in range(1, NZ):
            wait(rsz.at[d], rz_recv.at[d])
        total = sg[pl.ds(al(z, 64), 64), :]
        for d in range(1, NZ):
            total = total + rsz[d]
        acc1[...] = total
        for d in range(1, NY):
            other, device = at_y(d)
            send(acc1.at[pl.ds(al(other, 16), 16), :], rsy.at[d], ry_send.at[d], ry_recv.at[d], device)

    def grads_along_x():
        for d in range(1, NY):
            wait(rsy.at[d], ry_recv.at[d])
        total = acc1[pl.ds(al(y, 16), 16), :]
        for d in range(1, NY):
            total = total + rsy[d]
        acc2[...] = total
        for d in range(1, NX):
            other, device = at_x(d)
            send(acc2.at[pl.ds(al(lax.rem(other, 2), 8), 8), :], rsx.at[d], rx_send.at[d], rx_recv.at[d], device)

    def grads_arrived():
        for d in range(1, NX):
            wait(rsx.at[d], rx_recv.at[d])
        total = acc2[pl.ds(al(xl, 8), 8), :]
        for d in range(1, NX):
            total = total + rsx[d]
        acc3[...] = total / BLOCK

    def band_backward(g):
        group = pl.ds(al(g, D), D)
        for j in range(REPEAT):
            columns = slice(j * CHIP, (j + 1) * CHIP)
            back = dot(kv[1, :, group], db[g, :, columns])
            slope = (probs[g, :, columns].astype(F32) * (back - stats[g, 2:3, columns])).astype(BF16)
            slopes[:, columns] = slope

        @pl.when(g == GROUPS - 2)
        def _():
            grads_along_y()

        @pl.when(g == GROUPS - 1)
        def _():
            grads_along_x()

        q = stacked_queries(g)
        others = 3 * CHIP
        grad_k = (dot(slopes[:others, :], q) * SCALE).astype(BF16)
        grad_v = dot_t(probs[g, :others, :], db[g]).astype(BF16)
        for slot in range(3):
            gsend[slot, g, 0] = grad_k[slot * CHIP : (slot + 1) * CHIP, :]
            gsend[slot, g, 1] = grad_v[slot * CHIP : (slot + 1) * CHIP, :]
        for slot in range(2):
            send(
                gsend.at[slot, g], grecv.at[xh, g], g_send.at[slot, g], g_recv.at[xh, g], (before, slot * 2 + core)
            )

        @pl.when(xh == 1)
        def _():
            send(gsend.at[2, g], grecv.at[2, g], g_send.at[2, g], g_recv.at[2, g], (ctx, core))

        own[0, g] = dot(slopes[others:, :], q) * SCALE
        own[1, g] = dot_t(probs[g, others:, :], db[g])
        grad_q = (gqb[g] + dot(kvt[0, g], slopes[...])) * SCALE
        for j in range(REPEAT):
            gqout[:, pl.ds(al(g * REPEAT + j, D), D)] = grad_q[:, j * CHIP : (j + 1) * CHIP].T.astype(BF16)
        give(gqout, gq_ref, g, 1)

    def finish(g):
        for slot in range(2):
            wait(grecv.at[slot, g], g_recv.at[slot, g])

        @pl.when(xh == 0)
        def _():
            wait(grecv.at[2, g], g_recv.at[2, g])
            for i in range(2):
                own[i, g] += grecv[2, g, i].astype(F32)

        for i, ref in enumerate((gk_ref, gv_ref)):
            total = own[i, g] + grecv[0, g, i].astype(F32) + grecv[1, g, i].astype(F32)
            row = i * GROUPS + g
            fin[g, i] = (total + acc3[row : row + 1, :]).astype(BF16)
            cols = pl.ds(al(core * GROUPS + g, D), D)
            send(fin.at[g, i, her_rows, :], ref.at[:, cols], f_send.at[i, g], f_recv.at[i, g], sister)
            local(fin.at[g, i, my_rows, :], ref.at[:, cols], f_local.at[i, g])

    send_ahead(0)
    send_group(0)
    send_ahead(1)
    exchange_cores()
    summaries_along_y()
    pass_on(0)
    summaries_along_z()

    def step(t, carry):
        @pl.when(t < GROUPS)
        def _():
            band_forward(t)

        @pl.when(t == 0)
        def _():
            summaries_arrived()
            wait(dob, do_recv)

        @pl.when(t < GROUPS)
        def _():
            summary_part(t)

        @pl.when(t == GROUPS - 1)
        def _():
            grads_along_z()

        @pl.when(t != GROUPS - 2)
        def _():
            band_backward(t - lax.div(t, GROUPS - 1))

        return carry

    lax.fori_loop(0, GROUPS + 1, step, 0)
    grads_arrived()
    for g in range(GROUPS):
        finish(g)

    rows_all = kv.at[:, pl.ds(0, ROWS), :]
    wait(rows_all, kv_send.at[0])
    wait(qb.at[my_rows, :], q_send)

    @pl.when(xl == 1)
    def _():
        wait(kvl, st_send)

    wait(dob.at[my_rows, :], do_send)
    for h in range(4):
        wait(rows_all, kv_send.at[3 + h])

    @pl.when(xh == 0)
    def _():
        for c in range(2):
            wait(rows_all, kv_send.at[1 + c])

    @pl.when(xh == 1)
    def _():
        for g in range(GROUPS):
            wait(gsend.at[2, g], g_send.at[2, g])

    part = qb.at[my_rows, pl.ds(0, REPEAT * D)]
    for g in range(GROUPS):
        for slot in range(2):
            wait(gsend.at[slot, g], g_send.at[slot, g])
        for i in range(2):
            wait(part, o_send.at[i, g])
            wait(part, o_recv.at[i, g])
            wait(part, o_local.at[i, g])
            wait(fin.at[g, i, my_rows, :], f_send.at[i, g])
            wait(fin.at[g, i, my_rows, :], f_recv.at[i, g])
            wait(fin.at[g, i, my_rows, :], f_local.at[i, g])
    for d in range(1, NX):
        wait(rsx.at[d], rx_send.at[d])
    for slot in range(1, 2 * NX):
        wait(xs.at[slot], xs_send.at[slot])
    for d in range(1, NY):
        wait(rsy.at[d], ys_send.at[d])
        wait(rsy.at[d], ry_send.at[d])
    for d in range(1, NZ):
        wait(rsz.at[d], zs_send.at[d])
        wait(rsz.at[d], rz_send.at[d])


def deliver(*refs):
    sources, targets, held, fetched, stored = refs[:4], refs[4:8], refs[8:12], refs[12], refs[13]
    fetches = [pltpu.make_async_copy(sources[i], held[i], fetched.at[i]) for i in range(4)]
    stores = [pltpu.make_async_copy(held[i], targets[i], stored.at[i]) for i in range(4)]
    for copy in fetches:
        copy.start()
    for fetch, store in zip(fetches, stores):
        fetch.wait()
        store.start()
    for store in stores:
        store.wait()


def shards(queries, keys, values, cotangent):
    dma = pltpu.SemaphoreType.DMA
    scratch = [
        pltpu.VMEM((CHIP, QCOLS), BF16),
        pltpu.VMEM((CHIP, QCOLS), BF16),
        pltpu.VMEM((2, BAND, KCOLS), BF16),
        pltpu.VMEM((2, GROUPS, D, BAND), BF16),
        pltpu.VMEM((GROUPS, BAND, REPEAT * CHIP), BF16),
        pltpu.VMEM((BAND, REPEAT * CHIP), BF16),
        pltpu.VMEM((GROUPS, D, REPEAT * CHIP), F32),
        pltpu.VMEM((GROUPS, D, REPEAT * CHIP), F32),
        pltpu.VMEM((GROUPS, D, REPEAT * CHIP), BF16),
        pltpu.VMEM((GROUPS, 8, REPEAT * CHIP), F32),
        pltpu.VMEM((CHIP, QCOLS), BF16),
        pltpu.VMEM((CHIP, QCOLS), BF16),
        pltpu.VMEM((2, ROWS, 2 * KCOLS), BF16),
        pltpu.VMEM((2, ROWS, 2 * KCOLS), BF16),
        pltpu.VMEM((2, 8, D), F32),
        pltpu.VMEM((2 * NX, 8, D), F32),
        pltpu.VMEM((NCTX * 8, D), F32),
        pltpu.VMEM((NCTX * 8, D), F32),
        pltpu.VMEM((NZ, 64, D), F32),
        pltpu.VMEM((NY, 16, D), F32),
        pltpu.VMEM((NX, 8, D), F32),
        pltpu.VMEM((64, D), F32),
        pltpu.VMEM((16, D), F32),
        pltpu.VMEM((8, D), F32),
        pltpu.VMEM((2, GROUPS, CHIP, D), F32),
        pltpu.VMEM((3, GROUPS, 2, CHIP, D), BF16),
        pltpu.VMEM((3, GROUPS, 2, CHIP, D), BF16),
        pltpu.VMEM((GROUPS, 2, CHIP, D), BF16),
        dma((2,)), dma, dma((GROUPS,)), dma((7,)), dma((4, GROUPS)),
        dma, dma, dma, dma, dma,
        dma((2 * NX,)), dma((2 * NX,)), dma((NY,)), dma((NY,)), dma((NZ,)), dma((NZ,)),
        dma((NZ,)), dma((NZ,)), dma((NY,)), dma((NY,)), dma((NX,)), dma((NX,)),
        dma((3, GROUPS)), dma((3, GROUPS)),
        dma((2, GROUPS)), dma((2, GROUPS)), dma((2, GROUPS)),
        dma((2, GROUPS)), dma((2, GROUPS)), dma((2, GROUPS)),
    ]
    anywhere = pl.BlockSpec(memory_space=pl.ANY)
    results = pl.pallas_call(
        kernel,
        out_shape=[jax.ShapeDtypeStruct(a.shape, BF16) for a in (queries, cotangent, keys, values)],
        in_specs=[anywhere] * 4,
        out_specs=[anywhere] * 4,
        scratch_shapes=scratch,
        compiler_params=pltpu.CompilerParams(
            collective_id=0, has_side_effects=True, vmem_limit_bytes=56 * 1024 * 1024
        ),
    )(queries, keys, values, cotangent)
    return pl.pallas_call(
        deliver,
        out_shape=[jax.ShapeDtypeStruct(a.shape, BF16) for a in results],
        in_specs=[anywhere] * 4,
        out_specs=[anywhere] * 4,
        scratch_shapes=[pltpu.VMEM(a.shape, BF16) for a in results] + [dma((4,)), dma((4,))],
    )(*results)


def solution(mesh):
    placed = P(("ctx", "head"), None)
    return jax.shard_map(
        shards, mesh=mesh, in_specs=(placed,) * 4, out_specs=(placed,) * 4, check_vma=False
    )
```

```python
import math

import jax
import jax.numpy as jnp
from jax import lax
from jax.experimental import pallas as pl
from jax.experimental.pallas import tpu as pltpu
from jax.sharding import PartitionSpec as P

MESH = pl.DeviceIdType.MESH
F32 = jnp.float32
BF16 = jnp.bfloat16

D = 128
BLOCK = 512
ROWS = 128
CHIP = 256
GROUPS = 4
REPEAT = 4
KCOLS = GROUPS * D
QCOLS = GROUPS * REPEAT * D
BAND = 4 * CHIP
NX, NY, NZ = 4, 4, 8
NCTX = 64
LOWEST = -1e30
SCALE = 1.0 / math.sqrt(D)
LOG2 = SCALE / math.log(2.0)


def dot(a, b):
    return jnp.dot(a, b, preferred_element_type=F32)


def dot_t(a, b):
    return lax.dot_general(a, b, (((1,), (1,)), ((), ())), preferred_element_type=F32)


def al(index, size):
    return pl.multiple_of(index * size, size)


def kernel(
    q_in, k_in, v_in, do_in, out_ref, gq_ref, gk_ref, gv_ref,
    qb, dob, kv, kvt, probs, slopes, ob, gqb, db, stats, outb, gqout,
    kvl, stage, sums, xs, sumb, sg, low, summary, sglow, rsz, rsy, rsx, acc1, acc2, acc3,
    own, gsend, grecv, fin,
    l_sem, st_send, st_recv, kv_send, kv_recv, own_recv, q_send, do_send, q_recv, do_recv,
    xs_send, xs_recv, ys_send, ys_recv, zs_send, zs_recv,
    rz_send, rz_recv, ry_send, ry_recv, rx_send, rx_recv,
    g_send, g_recv, o_send, o_recv, o_local, f_send, f_recv, f_local,
):
    ctx = lax.axis_index("ctx")
    head = lax.axis_index("head")
    core = lax.rem(head, 2)
    xh = lax.div(head, 2)
    xl = lax.rem(ctx, 2)
    y = lax.rem(lax.div(ctx, 2), NY)
    z = lax.div(ctx, 2 * NY)
    x = xh * 2 + xl
    sister = (ctx, xh * 2 + 1 - core)
    after = lax.rem(ctx + 1, NCTX)
    before = lax.rem(ctx + NCTX - 1, NCTX)
    onward = lax.rem(ctx + 2, NCTX)
    behind = lax.rem(ctx + NCTX - 2, NCTX)

    def at_x(d):
        other = lax.rem(x + d, NX)
        return other, (z * (2 * NY) + y * 2 + lax.rem(other, 2), lax.div(other, 2) * 2 + core)

    def at_y(d):
        other = lax.rem(y + d, NY)
        return other, (z * (2 * NY) + other * 2 + xl, head)

    def at_z(d):
        other = lax.rem(z + d, NZ)
        return other, (other * (2 * NY) + y * 2 + xl, head)

    def send(src, dst, send_sem, recv_sem, device):
        pltpu.make_async_remote_copy(
            src_ref=src, dst_ref=dst, send_sem=send_sem, recv_sem=recv_sem, device_id=device, device_id_type=MESH
        ).start()

    def local(src, dst, sem):
        pltpu.make_async_copy(src, dst, sem).start()

    def wait(ref, sem):
        pltpu.make_async_copy(ref, ref, sem).wait()

    my_rows = pl.ds(al(core, ROWS), ROWS)
    her_rows = pl.ds(al(1 - core, ROWS), ROWS)

    barrier = pltpu.get_barrier_semaphore()
    partners = [sister]
    partners += [(ctx, (1 - xh) * 2 + c) for c in range(2)]
    partners += [(c, h) for c in (after, before) for h in range(4)]
    partners += [(onward, head), (behind, head)]
    partners += [at_y(d)[1] for d in range(1, NY)] + [at_z(d)[1] for d in range(1, NZ)]
    for device in partners:
        pl.semaphore_signal(barrier, inc=1, device_id=device, device_id_type=MESH)

    for i, ref in enumerate((k_in, v_in)):
        local(ref, kvl.at[i], l_sem.at[i])

    for i, ref in enumerate((k_in, v_in)):
        local(ref.at[:, pl.ds(al(core, KCOLS), KCOLS)], kv.at[i, pl.ds(al(6 + core, ROWS), ROWS), :], own_recv)
    for ref, buf, sem in ((q_in, qb, q_recv), (do_in, dob, do_recv)):
        local(ref.at[:, pl.ds(al(core, QCOLS), QCOLS)], buf.at[my_rows, :], sem)

    @pl.when(xh == 0)
    def _():
        kv[:, 2 * CHIP : 3 * CHIP, :] = jnp.zeros((2, CHIP, KCOLS), BF16)

    pieces = ([], [])
    for i in range(2):
        wait(kvl.at[i], l_sem.at[i])
        total = jnp.sum(kvl[i].astype(F32), axis=0, keepdims=True)
        for half in range(2):
            pieces[half].extend(total[:, (half * GROUPS + g) * D : (half * GROUPS + g + 1) * D] for g in range(GROUPS))
    for half in range(2):
        sums[half] = jnp.concatenate(pieces[half], axis=0)
    xs[0] = sums[core]
    pl.semaphore_wait(barrier, len(partners))
    for d in range(NX):
        for other in range(2):
            if d + other > 0:
                half = 1 - core if other else core
                ctx_x, head_x = at_x(d)[1]
                slot = 2 * d + other
                device = (ctx_x, head_x - core + half)
                send(sums.at[half], xs.at[slot], xs_send.at[slot], xs_recv.at[slot], device)

    def send_kv(src, g, slot, half, sem, device):
        send(
            src.at[:, :, pl.ds(al(half * GROUPS + g, D), D)],
            kv.at[:, pl.ds(al(slot * 2 + core, ROWS), ROWS), pl.ds(al(g, D), D)],
            kv_send.at[sem],
            kv_recv.at[slot, g],
            device,
        )

    def send_ahead(g):
        @pl.when(xl == 1)
        def _():
            for half in range(2):
                cols = pl.ds(al(half * GROUPS + g, D), D)
                send(kvl.at[:, :, cols], stage.at[:, :, cols], st_send, st_recv.at[g], (onward, head))

    def send_group(g):
        @pl.when(xl == 0)
        def _():
            for h in range(4):
                send_kv(kvl, g, xh, h % 2, 3 + h, (after, h))

        @pl.when(xh == 0)
        def _():
            for c in range(2):
                send_kv(kvl, g, 2, c, 1 + c, (ctx, 2 + c))

    def pass_on(g):
        @pl.when(xl == 1)
        def _():
            wait(stage.at[:, :, pl.ds(0, 2 * D)], st_recv.at[g])
            for h in range(4):
                send_kv(stage, g, xh, h % 2, 3 + h, (before, h))

    def exchange_cores():
        send(
            kvl.at[:, :, pl.ds(al(1 - core, KCOLS), KCOLS)],
            kv.at[:, pl.ds(al(6 + core, ROWS), ROWS), :],
            kv_send.at[0], own_recv, sister,
        )
        her_cols = pl.ds(al(1 - core, QCOLS), QCOLS)
        send(q_in.at[:, her_cols], qb.at[my_rows, :], q_send, q_recv, sister)
        send(do_in.at[:, her_cols], dob.at[my_rows, :], do_send, do_recv, sister)

    def summaries_along_y():
        for slot in range(1, 2 * NX):
            wait(xs.at[slot], xs_recv.at[slot])
        mine = (xs[0] + xs[1] + xs[4] + xs[5]) / BLOCK
        others = (xs[2] + xs[3] + xs[6] + xs[7]) / BLOCK
        first = z * (2 * NY) + y * 2
        sumb[pl.ds(al(first + xl, 8), 8), :] = mine.astype(BF16).astype(F32)
        sumb[pl.ds(al(first + 1 - xl, 8), 8), :] = others.astype(BF16).astype(F32)
        rows = pl.ds(al(z * NY + y, 16), 16)
        for d in range(1, NY):
            send(sumb.at[rows, :], sumb.at[rows, :], ys_send.at[d], ys_recv.at[d], at_y(d)[1])

    def summaries_along_z():
        for d in range(1, NY):
            wait(sumb.at[pl.ds(0, 16), :], ys_recv.at[d])
        rows = pl.ds(al(z, 64), 64)
        low[rows, :] = sumb[rows, :].astype(BF16)
        for d in range(1, NZ):
            send(low.at[rows, :], low.at[rows, :], zs_send.at[d], zs_recv.at[d], at_z(d)[1])

    def summaries_arrived():
        for d in range(1, NZ):
            wait(low.at[pl.ds(0, 64), :], zs_recv.at[d])
        summary[...] = low[...].astype(F32)

    no_before = jnp.where(ctx == 0, LOWEST, 0.0).astype(F32)
    no_partner = jnp.where(xh == 0, LOWEST, 0.0).astype(F32)
    causal = lax.broadcasted_iota(jnp.int32, (CHIP, CHIP), 0) <= lax.broadcasted_iota(jnp.int32, (CHIP, CHIP), 1)

    def band_forward(g):
        group = pl.ds(al(g, D), D)
        @pl.when(g == 0)
        def _():
            wait(kv.at[:, pl.ds(3 * CHIP, CHIP), :], own_recv)
            wait(qb, q_recv)

        for slot in range(2):
            wait(kv.at[:, pl.ds(slot * CHIP, CHIP), group], kv_recv.at[slot, g])

        @pl.when(xh == 1)
        def _():
            wait(kv.at[:, pl.ds(2 * CHIP, CHIP), group], kv_recv.at[2, g])

        @pl.when(g + 1 < GROUPS)
        def _():
            send_group(g + 1)
            pass_on(g + 1)

        @pl.when(g + 2 < GROUPS)
        def _():
            send_ahead(g + 2)

        for i in range(2):
            kvt[i, g] = kv[i, :, group].T

        for j in range(REPEAT):
            columns = slice(j * CHIP, (j + 1) * CHIP)
            q = qb[:, pl.ds(al(g * REPEAT + j, D), D)]
            s = dot_t(kv[0, :, group], q)
            s_before, s_partner = s[: 2 * CHIP], s[2 * CHIP : 3 * CHIP]
            s_own = jnp.where(causal, s[3 * CHIP :], LOWEST)
            top = jnp.maximum(
                jnp.maximum(
                    jnp.max(s_before, axis=0, keepdims=True) + no_before,
                    jnp.max(s_partner, axis=0, keepdims=True) + no_partner,
                ),
                jnp.max(s_own, axis=0, keepdims=True),
            ) * LOG2
            w_before = jnp.exp2(s_before * LOG2 - (top - no_before))
            w_partner = jnp.exp2(s_partner * LOG2 - (top - no_partner))
            w_own = jnp.exp2(s_own * LOG2 - top)
            total = (
                jnp.sum(w_before, axis=0, keepdims=True)
                + jnp.sum(w_partner, axis=0, keepdims=True)
                + jnp.sum(w_own, axis=0, keepdims=True)
            )
            low = jnp.concatenate([w.astype(BF16) for w in (w_before, w_partner, w_own)], axis=0)
            probs[g, :, columns] = low
            ob[g, :, columns] = dot(kvt[1, g], low)
            stats[g, 0:1, columns] = top
            stats[g, 1:2, columns] = total

    seen = lax.broadcasted_iota(jnp.int32, (NCTX, REPEAT * CHIP), 0) < ctx

    def stacked_queries(g):
        return jnp.concatenate([qb[:, pl.ds(al(g * REPEAT + j, D), D)] for j in range(REPEAT)], axis=0)

    def summary_part(g):
        sum_k = summary[pl.ds(g, NCTX, stride=8), :]
        sum_v = summary[pl.ds(GROUPS + g, NCTX, stride=8), :]
        sum_kt, sum_vt = sum_k.T.astype(BF16), sum_v.T.astype(BF16)
        sum_k, sum_v = sum_k.astype(BF16), sum_v.astype(BF16)
        q = stacked_queries(g)
        s = jnp.where(seen, dot_t(sum_k, q), LOWEST)
        s_top = jnp.max(s, axis=0, keepdims=True) * LOG2
        w = jnp.where(seen, jnp.exp2(s * LOG2 - s_top), 0.0)
        b_top, b_total = stats[g, 0:1, :], stats[g, 1:2, :]
        top = jnp.maximum(s_top, b_top)
        b_part, s_part = jnp.exp2(b_top - top), jnp.exp2(s_top - top)
        inverse = 1.0 / (b_part * b_total + s_part * jnp.sum(w, axis=0, keepdims=True))
        b_part, s_part = b_part * inverse, s_part * inverse
        w_low = w.astype(BF16)
        attended = ob[g] * b_part + dot(sum_vt, w_low) * s_part
        grads = []
        for j in range(REPEAT):
            cols = pl.ds(al(g * REPEAT + j, D), D)
            outb[:, cols] = attended[:, j * CHIP : (j + 1) * CHIP].T.astype(BF16)
            grads.append(dob[:, cols].astype(F32).T)
        grad_out = jnp.concatenate(grads, axis=1)
        b_grad = (grad_out * (16.0 * b_part)).astype(BF16)
        s_grad = (grad_out * (16.0 * s_part)).astype(BF16)
        db[g] = b_grad
        stats[g, 2:3, :] = jnp.sum(b_grad.astype(F32) * attended, axis=0, keepdims=True)
        s_dot = jnp.sum(s_grad.astype(F32) * attended, axis=0, keepdims=True)
        slope = (w * (dot(sum_v, s_grad) - s_dot)).astype(BF16)
        gqb[g] = dot(sum_kt, slope)
        sg[pl.ds(g, NCTX, stride=8), :] = dot(slope, q) * SCALE
        sg[pl.ds(GROUPS + g, NCTX, stride=8), :] = dot_t(w_low, s_grad)
        give(outb, out_ref, g, 0)

    def give(buf, ref, g, which):
        cols = pl.ds(al(g, REPEAT * D), REPEAT * D)
        out_cols = pl.ds(al(core * GROUPS + g, REPEAT * D), REPEAT * D)
        send(buf.at[her_rows, cols], ref.at[:, out_cols], o_send.at[which, g], o_recv.at[which, g], sister)
        local(buf.at[my_rows, cols], ref.at[:, out_cols], o_local.at[which, g])

    def grads_along_z():
        sglow[...] = sg[...].astype(BF16)
        for d in range(1, NZ):
            other, device = at_z(d)
            send(sglow.at[pl.ds(al(other, 64), 64), :], rsz.at[d], rz_send.at[d], rz_recv.at[d], device)

    def grads_along_y():
        for d in range(1, NZ):
            wait(rsz.at[d], rz_recv.at[d])
        total = sg[pl.ds(al(z, 64), 64), :]
        for d in range(1, NZ):
            total = total + rsz[d].astype(F32)
        acc1[...] = total
        for d in range(1, NY):
            other, device = at_y(d)
            send(acc1.at[pl.ds(al(other, 16), 16), :], rsy.at[d], ry_send.at[d], ry_recv.at[d], device)

    def grads_along_x():
        for d in range(1, NY):
            wait(rsy.at[d], ry_recv.at[d])
        total = acc1[pl.ds(al(y, 16), 16), :]
        for d in range(1, NY):
            total = total + rsy[d]
        acc2[...] = total
        for d in range(1, NX):
            other, device = at_x(d)
            send(acc2.at[pl.ds(al(lax.rem(other, 2), 8), 8), :], rsx.at[d], rx_send.at[d], rx_recv.at[d], device)

    def grads_arrived():
        for d in range(1, NX):
            wait(rsx.at[d], rx_recv.at[d])
        total = acc2[pl.ds(al(xl, 8), 8), :]
        for d in range(1, NX):
            total = total + rsx[d]
        acc3[...] = total / BLOCK

    def band_backward(g):
        group = pl.ds(al(g, D), D)
        for j in range(REPEAT):
            columns = slice(j * CHIP, (j + 1) * CHIP)
            back = dot(kv[1, :, group], db[g, :, columns])
            slope = (probs[g, :, columns].astype(F32) * (back - stats[g, 2:3, columns])).astype(BF16)
            slopes[:, columns] = slope

        @pl.when(g == GROUPS - 2)
        def _():
            grads_along_y()

        @pl.when(g == GROUPS - 1)
        def _():
            grads_along_x()

        q = stacked_queries(g)
        others = 3 * CHIP
        grad_k = (dot(slopes[:others, :], q) * SCALE).astype(BF16)
        grad_v = dot_t(probs[g, :others, :], db[g]).astype(BF16)
        for slot in range(3):
            gsend[slot, g, 0] = grad_k[slot * CHIP : (slot + 1) * CHIP, :]
            gsend[slot, g, 1] = grad_v[slot * CHIP : (slot + 1) * CHIP, :]
        for slot in range(2):
            send(
                gsend.at[slot, g], grecv.at[xh, g], g_send.at[slot, g], g_recv.at[xh, g], (before, slot * 2 + core)
            )

        @pl.when(xh == 1)
        def _():
            send(gsend.at[2, g], grecv.at[2, g], g_send.at[2, g], g_recv.at[2, g], (ctx, core))

        own[0, g] = dot(slopes[others:, :], q) * SCALE
        own[1, g] = dot_t(probs[g, others:, :], db[g])
        grad_q = (gqb[g] + dot(kvt[0, g], slopes[...])) * SCALE
        for j in range(REPEAT):
            gqout[:, pl.ds(al(g * REPEAT + j, D), D)] = grad_q[:, j * CHIP : (j + 1) * CHIP].T.astype(BF16)
        give(gqout, gq_ref, g, 1)

    def finish(g):
        for slot in range(2):
            wait(grecv.at[slot, g], g_recv.at[slot, g])

        @pl.when(xh == 0)
        def _():
            wait(grecv.at[2, g], g_recv.at[2, g])
            for i in range(2):
                own[i, g] += grecv[2, g, i].astype(F32)

        for i, ref in enumerate((gk_ref, gv_ref)):
            total = own[i, g] + grecv[0, g, i].astype(F32) + grecv[1, g, i].astype(F32)
            row = i * GROUPS + g
            fin[g, i] = (total + acc3[row : row + 1, :]).astype(BF16)
            cols = pl.ds(al(core * GROUPS + g, D), D)
            send(fin.at[g, i, her_rows, :], ref.at[:, cols], f_send.at[i, g], f_recv.at[i, g], sister)
            local(fin.at[g, i, my_rows, :], ref.at[:, cols], f_local.at[i, g])

    send_ahead(0)
    send_group(0)
    exchange_cores()
    summaries_along_y()
    send_ahead(1)
    pass_on(0)
    summaries_along_z()

    def step(t, carry):
        @pl.when(t < GROUPS)
        def _():
            band_forward(t)

        @pl.when(t == 0)
        def _():
            summaries_arrived()
            wait(dob, do_recv)

        @pl.when(t < GROUPS)
        def _():
            summary_part(t)

        @pl.when(t == GROUPS - 1)
        def _():
            grads_along_z()

        @pl.when(t != GROUPS - 2)
        def _():
            band_backward(t - lax.div(t, GROUPS - 1))

        return carry

    lax.fori_loop(0, GROUPS + 1, step, 0)
    grads_arrived()
    for g in range(GROUPS):
        finish(g)

    rows_all = kv.at[:, pl.ds(0, ROWS), :]
    wait(rows_all, kv_send.at[0])
    wait(qb.at[my_rows, :], q_send)

    @pl.when(xl == 1)
    def _():
        wait(kvl, st_send)

    wait(dob.at[my_rows, :], do_send)
    for h in range(4):
        wait(rows_all, kv_send.at[3 + h])

    @pl.when(xh == 0)
    def _():
        for c in range(2):
            wait(rows_all, kv_send.at[1 + c])

    @pl.when(xh == 1)
    def _():
        for g in range(GROUPS):
            wait(gsend.at[2, g], g_send.at[2, g])

    part = qb.at[my_rows, pl.ds(0, REPEAT * D)]
    for g in range(GROUPS):
        for slot in range(2):
            wait(gsend.at[slot, g], g_send.at[slot, g])
        for i in range(2):
            wait(part, o_send.at[i, g])
            wait(part, o_recv.at[i, g])
            wait(part, o_local.at[i, g])
            wait(fin.at[g, i, my_rows, :], f_send.at[i, g])
            wait(fin.at[g, i, my_rows, :], f_recv.at[i, g])
            wait(fin.at[g, i, my_rows, :], f_local.at[i, g])
    for d in range(1, NX):
        wait(rsx.at[d], rx_send.at[d])
    for slot in range(1, 2 * NX):
        wait(xs.at[slot], xs_send.at[slot])
    for d in range(1, NY):
        wait(rsy.at[d], ys_send.at[d])
        wait(rsy.at[d], ry_send.at[d])
    for d in range(1, NZ):
        wait(rsz.at[d], zs_send.at[d])
        wait(rsz.at[d], rz_send.at[d])


def deliver(*refs):
    sources, targets, held, fetched, stored = refs[:4], refs[4:8], refs[8:12], refs[12], refs[13]
    fetches = [pltpu.make_async_copy(sources[i], held[i], fetched.at[i]) for i in range(4)]
    stores = [pltpu.make_async_copy(held[i], targets[i], stored.at[i]) for i in range(4)]
    for copy in fetches:
        copy.start()
    for fetch, store in zip(fetches, stores):
        fetch.wait()
        store.start()
    for store in stores:
        store.wait()


def shards(queries, keys, values, cotangent):
    dma = pltpu.SemaphoreType.DMA
    scratch = [
        pltpu.VMEM((CHIP, QCOLS), BF16),
        pltpu.VMEM((CHIP, QCOLS), BF16),
        pltpu.VMEM((2, BAND, KCOLS), BF16),
        pltpu.VMEM((2, GROUPS, D, BAND), BF16),
        pltpu.VMEM((GROUPS, BAND, REPEAT * CHIP), BF16),
        pltpu.VMEM((BAND, REPEAT * CHIP), BF16),
        pltpu.VMEM((GROUPS, D, REPEAT * CHIP), F32),
        pltpu.VMEM((GROUPS, D, REPEAT * CHIP), F32),
        pltpu.VMEM((GROUPS, D, REPEAT * CHIP), BF16),
        pltpu.VMEM((GROUPS, 8, REPEAT * CHIP), F32),
        pltpu.VMEM((CHIP, QCOLS), BF16),
        pltpu.VMEM((CHIP, QCOLS), BF16),
        pltpu.VMEM((2, ROWS, 2 * KCOLS), BF16),
        pltpu.VMEM((2, ROWS, 2 * KCOLS), BF16),
        pltpu.VMEM((2, 8, D), F32),
        pltpu.VMEM((2 * NX, 8, D), F32),
        pltpu.VMEM((NCTX * 8, D), F32),
        pltpu.VMEM((NCTX * 8, D), F32),
        pltpu.VMEM((NCTX * 8, D), BF16),
        pltpu.VMEM((NCTX * 8, D), F32),
        pltpu.VMEM((NCTX * 8, D), BF16),
        pltpu.VMEM((NZ, 64, D), BF16),
        pltpu.VMEM((NY, 16, D), F32),
        pltpu.VMEM((NX, 8, D), F32),
        pltpu.VMEM((64, D), F32),
        pltpu.VMEM((16, D), F32),
        pltpu.VMEM((8, D), F32),
        pltpu.VMEM((2, GROUPS, CHIP, D), F32),
        pltpu.VMEM((3, GROUPS, 2, CHIP, D), BF16),
        pltpu.VMEM((3, GROUPS, 2, CHIP, D), BF16),
        pltpu.VMEM((GROUPS, 2, CHIP, D), BF16),
        dma((2,)), dma, dma((GROUPS,)), dma((7,)), dma((4, GROUPS)),
        dma, dma, dma, dma, dma,
        dma((2 * NX,)), dma((2 * NX,)), dma((NY,)), dma((NY,)), dma((NZ,)), dma((NZ,)),
        dma((NZ,)), dma((NZ,)), dma((NY,)), dma((NY,)), dma((NX,)), dma((NX,)),
        dma((3, GROUPS)), dma((3, GROUPS)),
        dma((2, GROUPS)), dma((2, GROUPS)), dma((2, GROUPS)),
        dma((2, GROUPS)), dma((2, GROUPS)), dma((2, GROUPS)),
    ]
    anywhere = pl.BlockSpec(memory_space=pl.ANY)
    results = pl.pallas_call(
        kernel,
        out_shape=[jax.ShapeDtypeStruct(a.shape, BF16) for a in (queries, cotangent, keys, values)],
        in_specs=[anywhere] * 4,
        out_specs=[anywhere] * 4,
        scratch_shapes=scratch,
        compiler_params=pltpu.CompilerParams(
            collective_id=0, has_side_effects=True, vmem_limit_bytes=56 * 1024 * 1024
        ),
    )(queries, keys, values, cotangent)
    return pl.pallas_call(
        deliver,
        out_shape=[jax.ShapeDtypeStruct(a.shape, BF16) for a in results],
        in_specs=[anywhere] * 4,
        out_specs=[anywhere] * 4,
        scratch_shapes=[pltpu.VMEM(a.shape, BF16) for a in results] + [dma((4,)), dma((4,))],
    )(*results)


def solution(mesh):
    placed = P(("ctx", "head"), None)
    return jax.shard_map(
        shards, mesh=mesh, in_specs=(placed,) * 4, out_specs=(placed,) * 4, check_vma=False
    )
```
